128 devices in a mesh: gx: 16 (over y, x), gy: 8 (over z, core).
Axes of the slice: x: 4, y: 4, z: 4, core: 2. Of those that a mesh axis runs over, the one named last changes fastest.
Arguments:
- points_in: bfloat16 [1048576, 64], P(('gx', 'gy')), may hold values from -6 to 6
- tree_perm: int32 [1048576], P(('gx', 'gy')), may hold values from 0 to 8191, as said below
- basis: bfloat16 [4096, 256, 64], P(('gx', 'gy')), may hold values from -0.75 to 0.75
- transfer: bfloat16 [4096, 64, 64], P(('gx', 'gy')), may hold values from -0.75 to 0.75
- couple_fine: bfloat16 [65536, 64, 64], P(('gx', 'gy')), may hold values from -0.1875 to 0.1875
- couple_coarse: bfloat16 [32768, 64, 64], P(('gx', 'gy')), may hold values from -0.1875 to 0.1875
- list_fine: int32 [4096, 16], P(('gx', 'gy')), may hold values from 0 to 4095, as said below
- list_coarse: int32 [2048, 16], P(('gx', 'gy')), may hold values from 0 to 2047, as said below
- near_blocks: bfloat16 [16384, 256, 256], P(('gx', 'gy')), may hold values from -0.375 to 0.375
- near_target: int32 [16384], P(('gx', 'gy')), may hold values from 0 to 31
- near_source: int32 [16384], P(('gx', 'gy')), may hold values from 0 to 35
- task_count: int32 [128], P(('gx', 'gy')), may hold values from 32 to 128, as said below
Outputs:
- product: float32 [1048576, 64], P(('gx', 'gy'))
The draws below stay inside these ranges and needn't reach their ends.
Inputs may be any that keep to these rules, and one draw needn't show every extreme that they name: `tree_perm`: each device's slice of 8192 entries is a permutation of 0 to 8191. `list_fine`: devices are numbered in tree order, gx index times the size of gy plus gy index, each holding 32 consecutive leaves. Every entry of a device names a leaf of one of the nine devices at most one step away along gx and along gy, wrapping round, itself included; each of those nine is named by some entry of every device. `list_coarse`: likewise for parents, each device holding 16 consecutive parents: every entry names a parent of one of the nine devices at most one step away along gx and along gy, wrapping round, itself included; each of those nine is named by some entry of every device. `task_count`: some device is full in every draw.
All inputs are finite; a program needn't handle non-finite values.
Results may differ from the reference program's by a relative error of at most 0.0048.
Values may be sent and summed in bfloat16 or wider, within the bound.
No kernel may reach another device: no remote copies, remote signals or barrier semaphores. Data moves between devices by JAX's collectives and lax.ppermute only.
A program may use at most 192 MiB of HBM per device.

```python
import jax
import jax.numpy as jnp
from jax import lax

P_SIZE = 256
RIGHT_HAND_SIDES = 64
SKELETON_RANK = 64
NCPL = 16
W = 2
C0 = 32
TASK_DEV = 128
NLEAF = 4096
NPTS = 1048576
N_GX = 16
N_GY = 8
DEVICES = 128


def coupling_lists(key, clusters):
    devices = N_GX * N_GY
    entries = clusters * NCPL

    def per_device(device_key, device):
        first, second = jax.random.split(device_key, 2)
        order = jax.random.permutation(first, entries)
        slot = (jnp.arange(entries, dtype=jnp.int32) % 9)[order]
        step_x = slot // 3 - 1
        step_y = slot % 3 - 1
        outer = (device // N_GY + step_x + N_GX) % N_GX
        inner = (device % N_GY + step_y + N_GY) % N_GY
        owner = outer * N_GY + inner
        within = jax.random.randint(second, (entries,), 0, clusters, dtype=jnp.int32)
        return (owner * clusters + within).reshape(clusters, NCPL)
    keys = jax.random.split(key, devices)
    lists = jax.vmap(per_device)(keys, jnp.arange(devices, dtype=jnp.int32))
    return lists.reshape(devices * clusters, NCPL).astype(jnp.int32)


def draw_tree_perm(key, part):
    key = jax.random.fold_in(key, 11)
    devices = N_GX * N_GY
    block_rows = C0 * P_SIZE
    shuffled = jax.vmap(lambda device_key: jax.random.permutation(device_key, block_rows))(jax.random.split(key, devices))
    return shuffled.astype(jnp.int32).reshape(-1)


def draw_list_fine(key, part):
    key = jax.random.fold_in(key, 21)
    return coupling_lists(key, C0)


def draw_list_coarse(key, part):
    key = jax.random.fold_in(key, 22)
    return coupling_lists(key, C0 // 2)


def draw_task_count(key, part):
    key = jax.random.fold_in(key, 31)
    devices = N_GX * N_GY
    first, second, third = jax.random.split(key, 3)
    heavy = jax.random.randint(first, (devices,), 0, 3, dtype=jnp.int32) == 0
    light = jax.random.randint(second, (devices,), TASK_DEV // 4, TASK_DEV // 2 + 1, dtype=jnp.int32)
    counts = jnp.where(heavy, TASK_DEV, light).astype(jnp.int32)
    chosen = jax.random.randint(third, (), 0, devices, dtype=jnp.int32)
    return counts.at[chosen].set(TASK_DEV)


def plant(values, key, smallest, high):
    longest = values.shape.index(max(values.shape))
    spots = []
    for shift in (0, 1):
        where = [jax.random.randint(jax.random.fold_in(key, axis), (), 0, length) for axis, length in enumerate(values.shape)]
        where[longest] = (where[longest] + shift) % values.shape[longest]
        spots.append(tuple(where))
    return values.at[spots[0]].set(smallest).at[spots[1]].set(high)


def block_levels(stream_key, shape, cuts, low, top_value):
    gain = 1.0
    for dim, blocks in cuts:
        draws = jax.random.uniform(jax.random.fold_in(jax.random.fold_in(stream_key, 6), dim), (blocks,), jnp.float32, low / len(cuts), top_value / len(cuts))
        gain = gain * jnp.repeat(jnp.exp(draws), shape[dim] // blocks).reshape((-1,) + (1,) * (len(shape) - 1 - dim))
    return gain


def bell_draw(rng, extent, scale, bound, cuts=(), held_as=jnp.bfloat16):
    result = scale * jax.random.normal(rng, extent, jnp.float32)
    if cuts:
        result = result * block_levels(rng, extent, cuts, -0.22, 0.18)
    return jnp.clip(result, -bound, bound).astype(held_as)


def setup_inputs(seed: int = 0) -> dict:
    key_of = jax.random.split(jax.random.key(seed), 13)
    points_in = bell_draw(key_of[0], (NPTS, RIGHT_HAND_SIDES), 1.0, 6.0, ((0, 128),))
    tree_perm = draw_tree_perm(jax.random.fold_in(key_of[12], 71), 0)
    basis = bell_draw(key_of[2], (NLEAF, P_SIZE, SKELETON_RANK), SKELETON_RANK ** -0.5, 0.75, ((0, 128),))
    transfer = bell_draw(key_of[3], (NLEAF, SKELETON_RANK, SKELETON_RANK), SKELETON_RANK ** -0.5, 0.75, ((0, 128),))
    couple_fine = bell_draw(key_of[4], (NLEAF * NCPL, SKELETON_RANK, SKELETON_RANK), (SKELETON_RANK * NCPL) ** -0.5, 0.1875, ((0, 128),))
    couple_coarse = bell_draw(key_of[5], (NLEAF // 2 * NCPL, SKELETON_RANK, SKELETON_RANK), (SKELETON_RANK * NCPL) ** -0.5, 0.1875, ((0, 128),))
    list_fine = draw_list_fine(jax.random.fold_in(key_of[12], 71), 0)
    list_coarse = draw_list_coarse(jax.random.fold_in(key_of[12], 71), 0)
    near_blocks = bell_draw(key_of[8], (DEVICES * TASK_DEV, P_SIZE, P_SIZE), P_SIZE ** -0.5, 0.375, ((0, 128),))
    near_target = plant(jax.random.randint(key_of[9], (DEVICES * TASK_DEV,), 0, C0), jax.random.fold_in(key_of[9], 1), 0, C0 - 1).astype(jnp.int32)
    near_source = plant(jax.random.randint(key_of[10], (DEVICES * TASK_DEV,), 0, C0 + 2 * W), jax.random.fold_in(key_of[10], 1), 0, (C0 + 2 * W) - 1).astype(jnp.int32)
    task_count = draw_task_count(jax.random.fold_in(key_of[12], 71), 0)
    return {"points_in": points_in, "tree_perm": tree_perm, "basis": basis, "transfer": transfer, "couple_fine": couple_fine, "couple_coarse": couple_coarse, "list_fine": list_fine, "list_coarse": list_coarse, "near_blocks": near_blocks, "near_target": near_target, "near_source": near_source, "task_count": task_count}


def couple_level(skeleton, matrices, lists):
    clusters = lists.shape[0]

    def per_cluster(inputs):
        blocks, sources = inputs
        picked = skeleton[sources].astype(jnp.float32)
        return jnp.einsum("jkl,jlr->kr", blocks.astype(jnp.float32), picked, precision=lax.Precision.HIGHEST)

    return lax.map(per_cluster, (matrices.reshape(clusters, NCPL, SKELETON_RANK, SKELETON_RANK), lists))


def reference(points_in, tree_perm, basis, transfer, couple_fine, couple_coarse, list_fine, list_coarse, near_blocks, near_target, near_source, task_count):
    topmost_level = lax.Precision.HIGHEST
    devices = N_GX * N_GY
    leaf_clusters = devices * C0
    parent_clusters = leaf_clusters // 2
    block_rows = C0 * P_SIZE
    row_base = (jnp.arange(leaf_clusters * P_SIZE, dtype=jnp.int32) // block_rows) * block_rows
    global_rows = (row_base + tree_perm).astype(jnp.int32)
    ordered = points_in[global_rows]
    leaf_points = ordered.reshape(leaf_clusters, P_SIZE, RIGHT_HAND_SIDES)
    fine_skeleton = jnp.einsum("cpk,cpr->ckr", basis.astype(jnp.float32), leaf_points.astype(jnp.float32), precision=topmost_level).astype(jnp.bfloat16)
    cluster_pairs = transfer.reshape(parent_clusters, 2, SKELETON_RANK, SKELETON_RANK).astype(jnp.float32)
    coarse_skeleton = jnp.einsum("mzgh,mzgp->mhp", cluster_pairs, fine_skeleton.reshape(parent_clusters, 2, SKELETON_RANK, RIGHT_HAND_SIDES).astype(jnp.float32), precision=topmost_level).astype(jnp.bfloat16)
    local_fine = couple_level(fine_skeleton, couple_fine, list_fine)
    coarse_local_rows = couple_level(coarse_skeleton, couple_coarse, list_coarse).astype(jnp.bfloat16)
    forwarded_skeletons = jnp.einsum("ednx,exw->ednw", cluster_pairs, coarse_local_rows.astype(jnp.float32), precision=topmost_level).reshape(leaf_clusters, SKELETON_RANK, RIGHT_HAND_SIDES)
    local_leaf = (local_fine + forwarded_skeletons).astype(jnp.bfloat16)
    far_field = jnp.einsum("cpk,ckr->cpr", basis.astype(jnp.float32), local_leaf.astype(jnp.float32), precision=topmost_level)
    margin = jnp.zeros((W, P_SIZE, RIGHT_HAND_SIDES), jnp.bfloat16)
    padded = jnp.concatenate([margin, leaf_points, margin], axis=0)
    slot_ids = jnp.arange(TASK_DEV, dtype=jnp.int32)
    leaf_ids = jnp.arange(C0, dtype=jnp.int32)

    def per_device(carry, inputs):
        blocks, targets, sources, count, device = inputs
        window = lax.dynamic_slice_in_dim(padded, (device * C0).astype(jnp.int32), C0 + 2 * W, 0)
        gathered = window[sources].astype(jnp.float32)
        products = jnp.einsum("tpq,tqr->tpr", blocks.astype(jnp.float32), gathered, precision=topmost_level)
        live = (slot_ids < count).astype(jnp.float32)
        selector = (targets[:, None] == leaf_ids[None, :]).astype(jnp.float32) * live[:, None]
        return carry, jnp.einsum("tc,tpr->cpr", selector, products, precision=topmost_level)

    inputs = (near_blocks.reshape(devices, TASK_DEV, P_SIZE, P_SIZE), near_target.reshape(devices, TASK_DEV), near_source.reshape(devices, TASK_DEV), task_count, jnp.arange(devices, dtype=jnp.int32))
    near_field = lax.scan(per_device, jnp.zeros((), jnp.float32), inputs)[1].reshape(leaf_clusters, P_SIZE, RIGHT_HAND_SIDES)
    tree_result = (far_field + near_field).reshape(leaf_clusters * P_SIZE, RIGHT_HAND_SIDES)
    return jnp.zeros((leaf_clusters * P_SIZE, RIGHT_HAND_SIDES), jnp.float32).at[global_rows].set(tree_result)
```

```python
import jax
import jax.numpy as jnp
from jax import lax
from jax.experimental import pallas as pl
from jax.experimental.pallas import tpu as pltpu
from jax.sharding import PartitionSpec as P

LEAVES = 32
PARENTS = LEAVES // 2
POINTS = 256
RANK = 64
COLS = 64
ENTRIES = 16
HALO = 2
TASKS = 128
ROWS = LEAVES * POINTS
PAIRS = LEAVES // 2 + PARENTS // 2
TASK_STEP = 8
LEAF_STEP = 4

SMEM = pltpu.SMEM
VMEM = pltpu.VMEM
F32 = jnp.float32
BF16 = jnp.bfloat16


def params(mib):
    return pltpu.CompilerParams(vmem_limit_bytes=mib << 20)


def low_half(rows):
    return lax.broadcasted_iota(jnp.int32, (rows, 128), 1) < 64


def swap_halves(x):
    return jnp.concatenate([x[:, 64:], x[:, :64]], axis=1)


def order_kernel(perm, points, basis, transfer, ordered, skeleton, edges, table, even, odd, fine):
    for c in range(ROWS // 128):
        block = points[:, c * 128 : (c + 1) * 128].astype(F32)
        table[c * 128 : (c + 1) * 128, :] = jnp.concatenate([block, block], axis=0).T

    def gather(leaf, into):
        rows = perm.at[pl.ds(leaf * POINTS, POINTS)]
        for i in range(POINTS):
            into[i : i + 1, :] = table[pl.ds(rows[i], 1), :]

    def finish(leaf, source):
        block = source[...].astype(BF16)
        ordered[leaf] = block
        fine[leaf] = jnp.dot(basis[leaf], block, preferred_element_type=F32).astype(BF16)

    gather(0, even)

    def two_leaves(step, _):
        gather(2 * step + 1, odd)
        finish(2 * step, even)
        gather(jnp.minimum(2 * step + 2, LEAVES - 1), even)
        finish(2 * step + 1, odd)
        return 0

    lax.fori_loop(0, LEAVES // 2, two_leaves, 0)

    low = low_half(RANK)
    low_points = low_half(POINTS)
    for p in range(PARENTS):
        skeleton[p] = jnp.where(low, fine[2 * p], fine[2 * p + 1])
    for q in range(PARENTS // 2):
        coarse = []
        for p in (2 * q, 2 * q + 1):
            pair = transfer[2 * p : 2 * p + 2].reshape(2 * RANK, RANK)
            stacked = fine[2 * p : 2 * p + 2].reshape(2 * RANK, 128)
            coarse.append(
                lax.dot_general(
                    pair, stacked, (((0,), (0,)), ((), ())), preferred_element_type=F32
                ).astype(BF16)
            )
        skeleton[PARENTS + q] = jnp.where(low, coarse[0], coarse[1])
    edges[0] = jnp.where(low_points, ordered[0], ordered[1])
    edges[1] = jnp.where(low_points, ordered[LEAVES - 2], ordered[LEAVES - 1])


def order_points(points, perm, basis, transfer):
    return pl.pallas_call(
        order_kernel,
        out_shape=(
            jax.ShapeDtypeStruct((LEAVES, POINTS, 128), BF16),
            jax.ShapeDtypeStruct((PAIRS, RANK, 128), BF16),
            jax.ShapeDtypeStruct((2, POINTS, 128), BF16),
        ),
        in_specs=[
            pl.BlockSpec(memory_space=SMEM),
            pl.BlockSpec(memory_space=VMEM),
            pl.BlockSpec(memory_space=VMEM),
            pl.BlockSpec(memory_space=VMEM),
        ],
        out_specs=(pl.BlockSpec(memory_space=VMEM),) * 3,
        scratch_shapes=[
            pltpu.VMEM((ROWS, 128), F32),
            pltpu.VMEM((POINTS, 128), F32),
            pltpu.VMEM((POINTS, 128), F32),
            pltpu.VMEM((LEAVES, RANK, 128), BF16),
        ],
        compiler_params=params(24),
        name="order_points",
    )(perm, points, basis, transfer)


def turn_kernel(blocks, turned, table):
    half = RANK // 2
    for k in range(half):
        block = jnp.concatenate([blocks[k], blocks[k + half]], axis=0).astype(F32)
        table[pl.ds(k, 128, stride=half), :] = block.T
    low = low_half(half)
    for t in range(128 // ENTRIES):
        for j in range(0, ENTRIES, 2):
            first = table[pl.ds((t * ENTRIES + j) * half, half), :]
            second = table[pl.ds((t * ENTRIES + j + 1) * half, half), :]
            turned[t, :half, j * 64 : (j + 2) * 64] = jnp.where(
                low, first, pltpu.roll(second, 64, 1)
            ).astype(BF16)
            turned[t, half:, j * 64 : (j + 2) * 64] = jnp.where(
                low, pltpu.roll(first, 64, 1), second
            ).astype(BF16)


def turn_blocks(blocks):
    entries = blocks.shape[2]
    targets = 128 // ENTRIES
    return pl.pallas_call(
        turn_kernel,
        grid=(entries // 128,),
        out_shape=jax.ShapeDtypeStruct((entries // ENTRIES, RANK, ENTRIES * RANK), BF16),
        in_specs=[pl.BlockSpec((RANK, RANK, 128), lambda i: (0, 0, i))],
        out_specs=pl.BlockSpec((targets, RANK, ENTRIES * RANK), lambda i: (i, 0, 0)),
        scratch_shapes=[pltpu.VMEM((128 * RANK // 2, 128), F32)],
        compiler_params=params(24),
        cost_estimate=pl.CostEstimate(
            flops=0, bytes_accessed=12 * blocks.size, transcendentals=0
        ),
        name="turn_blocks",
    )(blocks)


def near_kernel(targets, sources, count, before, after, ordered, blocks, total, window, sem):
    step = pl.program_id(0)

    @pl.when(step == 0)
    def _():
        copy = pltpu.make_async_copy(ordered, window.at[pl.ds(HALO, LEAVES)], sem)
        copy.start()
        window[0] = before[...]
        window[1] = swap_halves(before[...])
        window[LEAVES + 2] = after[...]
        window[LEAVES + 3] = swap_halves(after[...])
        total[...] = jnp.zeros_like(total)
        copy.wait()

    for i in range(TASK_STEP):
        task = step * TASK_STEP + i
        target = jnp.where(task < count[0], targets[task], LEAVES)
        total[target] += jnp.dot(blocks[i], window[sources[task]], preferred_element_type=F32)


def near_field(targets, sources, count, before, after, ordered, blocks):
    return pl.pallas_call(
        near_kernel,
        grid=(TASKS // TASK_STEP,),
        out_shape=jax.ShapeDtypeStruct((LEAVES + 1, POINTS, 128), F32),
        in_specs=[
            pl.BlockSpec(memory_space=SMEM),
            pl.BlockSpec(memory_space=SMEM),
            pl.BlockSpec(memory_space=SMEM),
            pl.BlockSpec(memory_space=VMEM),
            pl.BlockSpec(memory_space=VMEM),
            pl.BlockSpec(memory_space=pl.ANY),
            pl.BlockSpec((TASK_STEP, POINTS, POINTS), lambda i: (i, 0, 0)),
        ],
        out_specs=pl.BlockSpec((LEAVES + 1, POINTS, 128), lambda i: (0, 0, 0)),
        scratch_shapes=[
            pltpu.VMEM((LEAVES + 2 * HALO, POINTS, 128), BF16),
            pltpu.SemaphoreType.DMA,
        ],
        compiler_params=params(24),
        cost_estimate=pl.CostEstimate(
            flops=2 * TASKS * POINTS * POINTS * 128,
            bytes_accessed=2 * TASKS * POINTS * POINTS,
            transcendentals=0,
        ),
        name="near_field",
    )(targets, sources, count, before, after, ordered, blocks)


def result_kernel(*refs):
    perm, slots = refs[:2]
    skeletons = refs[2:11]
    fine, coarse, transfer, basis, near, out, spread, rows, table = refs[11:]
    step = pl.program_id(0)

    @pl.when(step == 0)
    def _():
        low = low_half(RANK)
        for a in range(9):

            def unpack(p, _):
                pair = skeletons[a][p]
                swapped = swap_halves(pair)
                spread[a * 2 * PAIRS + 2 * p] = jnp.where(low, pair, swapped)
                spread[a * 2 * PAIRS + 2 * p + 1] = jnp.where(low, swapped, pair)
                return 0

            lax.fori_loop(0, PAIRS, unpack, 0, unroll=4)

    def coupled(matrix, first):
        picked = [spread[slots[first + j]] for j in range(ENTRIES)]
        return jnp.dot(matrix, jnp.concatenate(picked, axis=0), preferred_element_type=F32)

    for p in range(LEAF_STEP // 2):
        parent = step * (LEAF_STEP // 2) + p
        from_parent = coupled(coarse[p], (LEAVES + parent) * ENTRIES).astype(BF16)
        for z in range(2):
            c = 2 * p + z
            leaf = step * LEAF_STEP + c
            local = coupled(fine[c], leaf * ENTRIES)
            local += jnp.dot(transfer[c], from_parent, preferred_element_type=F32)
            far = lax.dot_general(
                basis[c],
                local.astype(BF16),
                (((0,), (0,)), ((), ())),
                preferred_element_type=F32,
            )
            rows[c] = far + near[c]
    for c in range(LEAF_STEP):
        places = perm.at[pl.ds((step * LEAF_STEP + c) * POINTS, POINTS)]
        for i in range(POINTS):
            table[pl.ds(places[i], 1), :] = rows[c, i : i + 1, :]

    @pl.when(step == pl.num_programs(0) - 1)
    def _():
        for c in range(ROWS // 128):
            out[:, c * 128 : (c + 1) * 128] = table[c * 128 : (c + 1) * 128, :COLS].T


def result(perm, slots, skeletons, fine, coarse, transfer, basis, near):
    whole = pl.BlockSpec((PAIRS, RANK, 128), lambda i: (0, 0, 0))
    parents = LEAF_STEP // 2
    return pl.pallas_call(
        result_kernel,
        grid=(LEAVES // LEAF_STEP,),
        out_shape=jax.ShapeDtypeStruct((COLS, ROWS), F32),
        in_specs=[
            pl.BlockSpec(memory_space=SMEM),
            pl.BlockSpec(memory_space=SMEM),
            *[whole] * 9,
            pl.BlockSpec((LEAF_STEP, RANK, ENTRIES * RANK), lambda i: (i, 0, 0)),
            pl.BlockSpec((parents, RANK, ENTRIES * RANK), lambda i: (i, 0, 0)),
            pl.BlockSpec((LEAF_STEP, RANK, RANK), lambda i: (i, 0, 0)),
            pl.BlockSpec((LEAF_STEP, RANK, POINTS), lambda i: (i, 0, 0)),
            pl.BlockSpec((LEAF_STEP, POINTS, 128), lambda i: (i, 0, 0)),
        ],
        out_specs=pl.BlockSpec((COLS, ROWS), lambda i: (0, 0)),
        scratch_shapes=[
            pltpu.VMEM((9 * 2 * PAIRS, RANK, 128), BF16),
            pltpu.VMEM((LEAF_STEP, POINTS, 128), F32),
            pltpu.VMEM((ROWS, 128), F32),
        ],
        compiler_params=params(40),
        name="result",
    )(perm, slots, *skeletons, fine, coarse, transfer, basis, near)


def swaps(count, odd):
    pairs = [((i + odd) % count, (i + odd + 1) % count) for i in range(0, count, 2)]
    return [(a, b) for a, b in pairs] + [(b, a) for a, b in pairs]


def swap(x, axis, odd):
    return lax.ppermute(x, axis, swaps(lax.axis_size(axis), odd))


def places(lists, clusters, first):
    outer, inner = lax.axis_size("gx"), lax.axis_size("gy")
    gx, gy = lax.axis_index("gx"), lax.axis_index("gy")
    owner = lists // clusters
    step_x = (owner // inner - gx + outer) % outer
    step_y = (owner % inner - gy + inner) % inner
    array_x = jnp.where(step_x == 0, 0, jnp.where((step_x == 1) == (gx % 2 == 0), 1, 2))
    array_y = jnp.where(step_y == 0, 0, jnp.where((step_y == 1) == (gy % 2 == 0), 1, 2))
    return (array_x * 3 + array_y) * (2 * PAIRS) + first + lists % clusters


def on_device(
    points_in,
    tree_perm,
    basis,
    transfer,
    couple_fine,
    couple_coarse,
    list_fine,
    list_coarse,
    near_blocks,
    near_target,
    near_source,
    task_count,
):
    basis_rows = basis.transpose(0, 2, 1)
    slots = jnp.concatenate(
        [
            places(list_fine, LEAVES, 0).reshape(-1),
            places(list_coarse, PARENTS, LEAVES).reshape(-1),
        ]
    )
    ordered, own, edges = order_points(points_in.T, tree_perm, basis_rows, transfer)
    x_even = swap(own, "gx", 0)
    x_odd = swap(own, "gx", 1)
    y_even = swap(own, "gy", 0)
    y_odd = swap(own, "gy", 1)
    both = ("gx", "gy")
    last = lax.axis_size(both) - 1
    before = lax.ppermute(edges[1], both, [(i, i + 1) for i in range(last)])
    after = lax.ppermute(edges[0], both, [(i + 1, i) for i in range(last)])
    fine = turn_blocks(couple_fine.transpose(1, 2, 0))
    coarse = turn_blocks(couple_coarse.transpose(1, 2, 0))
    near = near_field(near_target, near_source, task_count, before, after, ordered, near_blocks)
    skeletons = [own, y_even, y_odd]
    for x in (x_even, x_odd):
        skeletons += [x, swap(x, "gy", 0), swap(x, "gy", 1)]
    out = result(tree_perm, slots, skeletons, fine, coarse, transfer, basis_rows, near)
    return out.T


def solution(mesh):
    flat = P(("gx", "gy"))
    return jax.shard_map(
        on_device,
        mesh=mesh,
        in_specs=(flat,) * 12,
        out_specs=flat,
        check_vma=False,
    )
```

```python
import jax
import jax.numpy as jnp
from jax import lax
from jax.experimental import pallas as pl
from jax.experimental.pallas import tpu as pltpu
from jax.sharding import PartitionSpec as P

LEAVES = 32
PARENTS = LEAVES // 2
POINTS = 256
RANK = 64
COLS = 64
ENTRIES = 16
HALO = 2
TASKS = 128
ROWS = LEAVES * POINTS
PAIRS = LEAVES // 2 + PARENTS // 2
TASK_STEP = 16
LEAF_STEP = 4
CHUNK = 1024
POINT_PARTS = 4
OUT_PARTS = 8
ORDER_MIB = 60
NEAR_MIB = 48
HELD = 4
PITCH = RANK // 2 + 1

SMEM = pltpu.SMEM
VMEM = pltpu.VMEM
F32 = jnp.float32
BF16 = jnp.bfloat16


def params(mib):
    return pltpu.CompilerParams(vmem_limit_bytes=mib << 20)


def low_half(rows):
    return lax.broadcasted_iota(jnp.int32, (rows, 128), 1) < 64


def swap_halves(x):
    return jnp.concatenate([x[:, 64:], x[:, :64]], axis=1)


def order_kernel(
    perm,
    points,
    basis,
    transfer,
    ordered,
    skeleton,
    edges,
    table,
    even,
    odd,
    fine,
    first_rows,
    second_rows,
    points_here,
    basis_here,
    transfer_here,
    ordered_here,
    sems,
    out_sems,
):
    width = ROWS // POINT_PARTS

    def part(n):
        span = pl.ds(n * width, width)
        return pltpu.make_async_copy(points.at[:, span], points_here.at[:, span], sems.at[n])

    def load_rows(chunk, into, sem):
        return pltpu.make_async_copy(
            perm.at[pl.ds(chunk * CHUNK, CHUNK)], into, sems.at[POINT_PARTS + sem]
        )

    for n in range(POINT_PARTS):
        part(n).start()
    load_rows(0, first_rows, 0).start()
    load_rows(1, second_rows, 1).start()
    bases = pltpu.make_async_copy(basis, basis_here, sems.at[POINT_PARTS + 2])
    transfers = pltpu.make_async_copy(transfer, transfer_here, sems.at[POINT_PARTS + 3])
    bases.start()
    transfers.start()
    for n in range(POINT_PARTS):
        part(n).wait()
        for c in range(n * width // 128, (n + 1) * width // 128):
            block = points_here[:, c * 128 : (c + 1) * 128].astype(F32)
            table[c * 128 : (c + 1) * 128, :] = jnp.concatenate([block, block], axis=0).T
    bases.wait()

    leaves = CHUNK // POINTS

    def gather(places, into):
        for i in range(CHUNK):
            into[i : i + 1, :] = table[pl.ds(places[i], 1), :]

    def finish(chunk, source):
        for n in range(leaves):
            leaf = chunk * leaves + n
            block = source[n * POINTS : (n + 1) * POINTS, :].astype(BF16)
            ordered_here[leaf] = block
            fine[leaf] = jnp.dot(basis_here[leaf], block, preferred_element_type=F32).astype(BF16)

    def send(chunk):
        span = pl.ds(chunk * leaves, leaves)
        return pltpu.make_async_copy(ordered_here.at[span], ordered.at[span], out_sems.at[chunk])

    chunks = ROWS // CHUNK
    load_rows(0, first_rows, 0).wait()
    gather(first_rows, even)

    def two_chunks(step, _):
        load_rows(2 * step + 1, second_rows, 1).wait()
        load_rows(2 * step + 2, first_rows, 0).start()
        finish(2 * step, even)
        gather(second_rows, odd)
        send(2 * step).start()

        load_rows(2 * step + 3, second_rows, 1).start()
        load_rows(2 * step + 2, first_rows, 0).wait()
        finish(2 * step + 1, odd)
        gather(first_rows, even)
        send(2 * step + 1).start()
        return 0

    lax.fori_loop(0, chunks // 2 - 1, two_chunks, 0)
    load_rows(chunks - 1, second_rows, 1).wait()
    finish(chunks - 2, even)
    gather(second_rows, odd)
    send(chunks - 2).start()
    finish(chunks - 1, odd)
    send(chunks - 1).start()

    transfers.wait()
    low = low_half(RANK)
    low_points = low_half(POINTS)
    for p in range(PARENTS):
        skeleton[p] = jnp.where(low, fine[2 * p], fine[2 * p + 1])
    for q in range(PARENTS // 2):
        coarse = []
        for p in (2 * q, 2 * q + 1):
            pair = transfer_here[2 * p : 2 * p + 2].reshape(2 * RANK, RANK)
            stacked = fine[2 * p : 2 * p + 2].reshape(2 * RANK, 128)
            coarse.append(
                lax.dot_general(
                    pair, stacked, (((0,), (0,)), ((), ())), preferred_element_type=F32
                ).astype(BF16)
            )
        skeleton[PARENTS + q] = jnp.where(low, coarse[0], coarse[1])
    edges[0] = jnp.where(low_points, ordered_here[0], ordered_here[1])
    edges[1] = jnp.where(low_points, ordered_here[LEAVES - 2], ordered_here[LEAVES - 1])
    for chunk in range(ROWS // CHUNK):
        send(chunk).wait()


def order_points(points, perm, basis, transfer):
    anywhere = pl.BlockSpec(memory_space=pl.ANY)
    return pl.pallas_call(
        order_kernel,
        out_shape=(
            jax.ShapeDtypeStruct((LEAVES, POINTS, 128), BF16),
            jax.ShapeDtypeStruct((PAIRS, RANK, 128), BF16),
            jax.ShapeDtypeStruct((2, POINTS, 128), BF16),
        ),
        in_specs=[anywhere] * 4,
        out_specs=(
            pl.BlockSpec(memory_space=pl.ANY),
            pl.BlockSpec(memory_space=VMEM),
            pl.BlockSpec(memory_space=VMEM),
        ),
        scratch_shapes=[
            pltpu.VMEM((ROWS, 128), F32),
            pltpu.VMEM((CHUNK, 128), F32),
            pltpu.VMEM((CHUNK, 128), F32),
            pltpu.VMEM((LEAVES, RANK, 128), BF16),
            pltpu.SMEM((CHUNK,), jnp.int32),
            pltpu.SMEM((CHUNK,), jnp.int32),
            pltpu.VMEM((COLS, ROWS), BF16),
            pltpu.VMEM((LEAVES, RANK, POINTS), BF16),
            pltpu.VMEM((LEAVES, RANK, RANK), BF16),
            pltpu.VMEM((LEAVES, POINTS, 128), BF16),
            pltpu.SemaphoreType.DMA((POINT_PARTS + 4,)),
            pltpu.SemaphoreType.DMA((ROWS // CHUNK,)),
        ],
        compiler_params=params(ORDER_MIB),
        name="order_points",
    )(perm, points, basis, transfer)


def turn_kernel(blocks, turned, table):
    half = RANK // 2
    targets = 128 // ENTRIES
    low = low_half(half)

    def tile(n, _):
        entries = pl.ds(pl.multiple_of(n * 128, 128), 128)
        for k in range(half):
            block = jnp.concatenate([blocks[k, :, entries], blocks[k + half, :, entries]], axis=0)
            table[pl.ds(k, 128, stride=PITCH), :] = block.astype(F32).T
        for t in range(targets):
            into = turned.at[n * targets + t]
            for j in range(0, ENTRIES, 2):
                first = table[pl.ds((t * ENTRIES + j) * PITCH, half), :]
                second = table[pl.ds((t * ENTRIES + j + 1) * PITCH, half), :]
                into[:half, j * 64 : (j + 2) * 64] = jnp.where(
                    low, first, pltpu.roll(second, 64, 1)
                ).astype(BF16)
                into[half:, j * 64 : (j + 2) * 64] = jnp.where(
                    low, pltpu.roll(first, 64, 1), second
                ).astype(BF16)
        return 0

    lax.fori_loop(0, blocks.shape[2] // 128, tile, 0)


def turn_blocks(blocks):
    return pl.pallas_call(
        turn_kernel,
        out_shape=jax.ShapeDtypeStruct((blocks.shape[2] // ENTRIES, RANK, ENTRIES * RANK), BF16),
        in_specs=[pl.BlockSpec(memory_space=VMEM)],
        out_specs=pl.BlockSpec(memory_space=VMEM),
        scratch_shapes=[pltpu.VMEM((128 * PITCH, 128), F32)],
        compiler_params=params(24),
        cost_estimate=pl.CostEstimate(
            flops=0, bytes_accessed=6 * blocks.size, transcendentals=0
        ),
        name="turn_blocks",
    )(blocks)


def near_kernel(
    targets, sources, count, before, after, ordered, blocks, total, window, held, sem, sems
):
    steps = TASKS // TASK_STEP

    def fetch(step):
        slot = lax.rem(step, HELD)
        tasks = pl.ds(step * TASK_STEP, TASK_STEP)
        return pltpu.make_async_copy(blocks.at[tasks], held.at[slot], sems.at[slot])

    copy = pltpu.make_async_copy(ordered, window.at[pl.ds(HALO, LEAVES)], sem)
    copy.start()
    for step in range(HELD - 1):
        fetch(step).start()
    low = low_half(POINTS)
    for pair, place in ((before[...], 0), (after[...], LEAVES + HALO)):
        swapped = swap_halves(pair)
        window[place] = jnp.where(low, pair, swapped)
        window[place + 1] = jnp.where(low, swapped, pair)
    total[...] = jnp.zeros_like(total)
    copy.wait()

    def one_step(step, _):
        slot = lax.rem(step, HELD)
        fetch(step).wait()

        @pl.when(step < steps - (HELD - 1))
        def _():
            fetch(step + HELD - 1).start()

        for i in range(TASK_STEP):
            task = step * TASK_STEP + i
            target = jnp.where(task < count[0], targets[task], LEAVES)
            total[target] += jnp.dot(
                held[slot, i], window[sources[task]], preferred_element_type=F32
            )
        return 0

    lax.fori_loop(0, steps, one_step, 0)


def near_field(targets, sources, count, before, after, ordered, blocks):
    return pl.pallas_call(
        near_kernel,
        out_shape=jax.ShapeDtypeStruct((LEAVES + 1, POINTS, 128), F32),
        in_specs=[
            pl.BlockSpec(memory_space=SMEM),
            pl.BlockSpec(memory_space=SMEM),
            pl.BlockSpec(memory_space=SMEM),
            pl.BlockSpec(memory_space=VMEM),
            pl.BlockSpec(memory_space=VMEM),
            pl.BlockSpec(memory_space=pl.ANY),
            pl.BlockSpec(memory_space=pl.ANY),
        ],
        out_specs=pl.BlockSpec(memory_space=VMEM),
        scratch_shapes=[
            pltpu.VMEM((LEAVES + 2 * HALO, POINTS, 128), BF16),
            pltpu.VMEM((HELD, TASK_STEP, POINTS, POINTS), BF16),
            pltpu.SemaphoreType.DMA,
            pltpu.SemaphoreType.DMA((HELD,)),
        ],
        compiler_params=params(NEAR_MIB),
        cost_estimate=pl.CostEstimate(
            flops=2 * TASKS * POINTS * POINTS * 128,
            bytes_accessed=2 * TASKS * POINTS * POINTS,
            transcendentals=0,
        ),
        name="near_field",
    )(targets, sources, count, before, after, ordered, blocks)


def result_kernel(*refs):
    perm, slots = refs[:2]
    skeletons = refs[2:11]
    fine, coarse, transfer, basis, near, out = refs[11:17]
    spread, below, above, first_rows, second_rows, table, wide = refs[17:24]
    first_places, second_places, sems, out_sems = refs[24:]
    steps = LEAVES // LEAF_STEP

    def load_places(step, into, sem):
        return pltpu.make_async_copy(perm.at[pl.ds(step * CHUNK, CHUNK)], into, sems.at[sem])

    load_places(0, first_places, 0).start()
    load_places(1, second_places, 1).start()
    low = low_half(RANK)
    keep = (low.astype(F32).astype(BF16), (~low).astype(F32).astype(BF16))
    for a in range(9):

        def part(p, _):
            for z in range(2):
                spread[a * 2 * PAIRS + 2 * p + z] = skeletons[a][p] * keep[z]
            return 0

        lax.fori_loop(0, PAIRS, part, 0, unroll=8)

    def coupled(matrix, first):
        picked = [spread[slots[first + j]] for j in range(ENTRIES)]
        return jnp.dot(matrix, jnp.concatenate(picked, axis=0), preferred_element_type=F32)

    def couple(step, _):
        for p in range(2):
            parent = step * 2 + p
            above[parent] = coupled(coarse[parent], (LEAVES + parent) * ENTRIES)
        for c in range(4):
            leaf = step * 4 + c
            below[leaf] = coupled(fine[leaf], leaf * ENTRIES)
        return 0

    lax.fori_loop(0, LEAVES // 4, couple, 0)

    def fold(halves):
        return halves + pltpu.roll(halves, 64, 1)

    def compute(step, rows):
        for p in range(LEAF_STEP // 2):
            parent = step * (LEAF_STEP // 2) + p
            from_parent = fold(above[parent]).astype(BF16)
            for z in range(2):
                c = 2 * p + z
                leaf = step * LEAF_STEP + c
                local = fold(below[leaf])
                local += jnp.dot(transfer[leaf], from_parent, preferred_element_type=F32)
                far = lax.dot_general(
                    basis[leaf],
                    local.astype(BF16),
                    (((0,), (0,)), ((), ())),
                    preferred_element_type=F32,
                )
                rows[c * POINTS : (c + 1) * POINTS, :] = far + near[leaf]

    def scatter(places, rows):
        for i in range(CHUNK):
            table[pl.ds(places[i], 1), :] = rows[i : i + 1, :]

    compute(0, first_rows)

    def two_steps(pair, _):
        load_places(2 * pair, first_places, 0).wait()
        compute(2 * pair + 1, second_rows)
        scatter(first_places, first_rows)
        more = pair < steps // 2 - 1

        @pl.when(more)
        def _():
            load_places(2 * pair + 2, first_places, 0).start()

        load_places(2 * pair + 1, second_places, 1).wait()
        compute(jnp.minimum(2 * pair + 2, steps - 1), first_rows)
        scatter(second_places, second_rows)

        @pl.when(more)
        def _():
            load_places(2 * pair + 3, second_places, 1).start()

        return 0

    lax.fori_loop(0, steps // 2, two_steps, 0)

    low = low_half(128)
    sends = []
    for n in range(OUT_PARTS):
        width = ROWS // OUT_PARTS
        for c in range(n * width // 128, (n + 1) * width // 128):
            block = table[c * 128 : (c + 1) * 128, :]
            high = block.astype(BF16)
            rest = (block - high.astype(F32)).astype(BF16)
            both = jnp.where(low, high, rest).T.astype(F32)
            wide[:, c * 128 : (c + 1) * 128] = both[:COLS] + both[COLS:]
        span = pl.ds(n * width, width)
        sends.append(pltpu.make_async_copy(wide.at[:, span], out.at[:, span], out_sems.at[n]))
        sends[-1].start()
    for send in sends:
        send.wait()


def result(perm, slots, skeletons, fine, coarse, transfer, basis, near):
    return pl.pallas_call(
        result_kernel,
        out_shape=jax.ShapeDtypeStruct((COLS, ROWS), F32),
        in_specs=[
            pl.BlockSpec(memory_space=pl.ANY),
            pl.BlockSpec(memory_space=SMEM),
            *[pl.BlockSpec(memory_space=VMEM)] * 14,
        ],
        out_specs=pl.BlockSpec(memory_space=pl.ANY),
        scratch_shapes=[
            pltpu.VMEM((9 * 2 * PAIRS, RANK, 128), BF16),
            pltpu.VMEM((LEAVES, RANK, 128), F32),
            pltpu.VMEM((PARENTS, RANK, 128), F32),
            pltpu.VMEM((CHUNK, 128), F32),
            pltpu.VMEM((CHUNK, 128), F32),
            pltpu.VMEM((ROWS, 128), F32),
            pltpu.VMEM((COLS, ROWS), F32),
            pltpu.SMEM((CHUNK,), jnp.int32),
            pltpu.SMEM((CHUNK,), jnp.int32),
            pltpu.SemaphoreType.DMA((2,)),
            pltpu.SemaphoreType.DMA((OUT_PARTS,)),
        ],
        compiler_params=params(36),
        name="result",
    )(perm, slots, *skeletons, fine, coarse, transfer, basis, near)


def swaps(count, odd):
    pairs = [((i + odd) % count, (i + odd + 1) % count) for i in range(0, count, 2)]
    return [(a, b) for a, b in pairs] + [(b, a) for a, b in pairs]


def swap(x, axis, odd):
    return lax.ppermute(x, axis, swaps(lax.axis_size(axis), odd))


def places(lists, clusters, first):
    outer, inner = lax.axis_size("gx"), lax.axis_size("gy")
    gx, gy = lax.axis_index("gx"), lax.axis_index("gy")
    owner = lists // clusters
    step_x = (owner // inner - gx + outer) % outer
    step_y = (owner % inner - gy + inner) % inner
    array_x = jnp.where(step_x == 0, 0, jnp.where((step_x == 1) == (gx % 2 == 0), 1, 2))
    array_y = jnp.where(step_y == 0, 0, jnp.where((step_y == 1) == (gy % 2 == 0), 1, 2))
    return (array_x * 3 + array_y) * (2 * PAIRS) + first + lists % clusters


def on_device(
    points_in,
    tree_perm,
    basis,
    transfer,
    couple_fine,
    couple_coarse,
    list_fine,
    list_coarse,
    near_blocks,
    near_target,
    near_source,
    task_count,
):
    basis_rows = basis.transpose(0, 2, 1)
    slots = jnp.concatenate(
        [
            places(list_fine, LEAVES, 0).reshape(-1),
            places(list_coarse, PARENTS, LEAVES).reshape(-1),
        ]
    )
    ordered, own, edges = order_points(points_in.T, tree_perm, basis_rows, transfer)
    x_even = swap(own, "gx", 0)
    x_odd = swap(own, "gx", 1)
    y_even = swap(own, "gy", 0)
    y_odd = swap(own, "gy", 1)
    both = ("gx", "gy")
    last = lax.axis_size(both) - 1
    before = lax.ppermute(edges[1], both, [(i, i + 1) for i in range(last)])
    after = lax.ppermute(edges[0], both, [(i + 1, i) for i in range(last)])
    fine = turn_blocks(couple_fine.transpose(1, 2, 0))
    coarse = turn_blocks(couple_coarse.transpose(1, 2, 0))
    near = near_field(near_target, near_source, task_count, before, after, ordered, near_blocks)
    skeletons = [own, y_even, y_odd]
    for x in (x_even, x_odd):
        skeletons += [x, swap(x, "gy", 0), swap(x, "gy", 1)]
    out = result(tree_perm, slots, skeletons, fine, coarse, transfer, basis_rows, near)
    return out.T


def solution(mesh):
    flat = P(("gx", "gy"))
    return jax.shard_map(
        on_device,
        mesh=mesh,
        in_specs=(flat,) * 12,
        out_specs=flat,
        check_vma=False,
    )
```

```python
import jax
import jax.numpy as jnp
from jax import lax
from jax.experimental import pallas as pl
from jax.experimental.pallas import tpu as pltpu
from jax.sharding import PartitionSpec as P

LEAVES = 32
PARENTS = LEAVES // 2
POINTS = 256
RANK = 64
COLS = 64
ENTRIES = 16
HALO = 2
TASKS = 128
ROWS = LEAVES * POINTS
PAIRS = LEAVES // 2 + PARENTS // 2
EDGE = POINTS // RANK
TASK_STEP = 16
LEAF_STEP = 4
CHUNK = 1024
POINT_PARTS = 4
OUT_PARTS = 8
ORDER_MIB = 60
NEAR_MIB = 36
HELD = 4
PITCH = RANK // 2 + 1

SMEM = pltpu.SMEM
VMEM = pltpu.VMEM
F32 = jnp.float32
BF16 = jnp.bfloat16


def params(mib):
    return pltpu.CompilerParams(vmem_limit_bytes=mib << 20)


def low_half(rows):
    return lax.broadcasted_iota(jnp.int32, (rows, 128), 1) < 64


def swap_halves(x):
    return jnp.concatenate([x[:, 64:], x[:, :64]], axis=1)


def places(lists, clusters, first):
    outer, inner = lax.axis_size("gx"), lax.axis_size("gy")
    gx, gy = lax.axis_index("gx"), lax.axis_index("gy")
    owner = lax.div(lists, clusters)
    step_x = lax.rem(lax.div(owner, inner) - gx + outer, outer)
    step_y = lax.rem(lax.rem(owner, inner) - gy + inner, inner)
    swap_x = jnp.where(step_x == 1, 1 + lax.rem(gx, 2), 2 - lax.rem(gx, 2))
    swap_y = jnp.where(step_y == 1, 1 + lax.rem(gy, 2), 2 - lax.rem(gy, 2))
    array = jnp.where(step_x == 0, 0, swap_x) * 3 + jnp.where(step_y == 0, 0, swap_y)
    return array * (2 * PAIRS) + first + lax.rem(lists, clusters)


def order_kernel(
    perm,
    points,
    basis,
    transfer,
    fine_lists,
    coarse_lists,
    ordered,
    skeleton,
    even_sent,
    odd_edge,
    fine_slots,
    coarse_slots,
    table,
    even,
    odd,
    fine,
    first_rows,
    second_rows,
    points_here,
    basis_here,
    transfer_here,
    ordered_here,
    sems,
    out_sems,
):
    width = ROWS // POINT_PARTS

    def part(n):
        span = pl.ds(n * width, width)
        return pltpu.make_async_copy(points.at[:, span], points_here.at[:, span], sems.at[n])

    def load_rows(chunk, into, sem):
        return pltpu.make_async_copy(
            perm.at[pl.ds(chunk * CHUNK, CHUNK)], into, sems.at[POINT_PARTS + sem]
        )

    for n in range(POINT_PARTS):
        part(n).start()
    load_rows(0, first_rows, 0).start()
    load_rows(1, second_rows, 1).start()
    bases = pltpu.make_async_copy(basis, basis_here, sems.at[POINT_PARTS + 2])
    transfers = pltpu.make_async_copy(transfer, transfer_here, sems.at[POINT_PARTS + 3])
    bases.start()
    transfers.start()
    for n in range(POINT_PARTS):
        part(n).wait()
        for c in range(n * width // 128, (n + 1) * width // 128):
            block = points_here[:, c * 128 : (c + 1) * 128].astype(F32)
            table[c * 128 : (c + 1) * 128, :] = jnp.concatenate([block, block], axis=0).T
    bases.wait()

    leaves = CHUNK // POINTS

    def gather(places, into):
        for i in range(CHUNK):
            into[i : i + 1, :] = table[pl.ds(places[i], 1), :]

    def finish(chunk, source):
        for n in range(leaves):
            leaf = chunk * leaves + n
            block = source[n * POINTS : (n + 1) * POINTS, :].astype(BF16)
            ordered_here[leaf] = block
            fine[leaf] = jnp.dot(basis_here[leaf], block, preferred_element_type=F32).astype(BF16)

    def send(chunk):
        span = pl.ds(chunk * leaves, leaves)
        return pltpu.make_async_copy(ordered_here.at[span], ordered.at[span], out_sems.at[chunk])

    chunks = ROWS // CHUNK
    load_rows(0, first_rows, 0).wait()
    gather(first_rows, even)

    def two_chunks(step, _):
        load_rows(2 * step + 1, second_rows, 1).wait()
        load_rows(2 * step + 2, first_rows, 0).start()
        finish(2 * step, even)
        gather(second_rows, odd)
        send(2 * step).start()

        load_rows(2 * step + 3, second_rows, 1).start()
        load_rows(2 * step + 2, first_rows, 0).wait()
        finish(2 * step + 1, odd)
        gather(first_rows, even)
        send(2 * step + 1).start()
        return 0

    lax.fori_loop(0, chunks // 2 - 1, two_chunks, 0)
    load_rows(chunks - 1, second_rows, 1).wait()
    finish(chunks - 2, even)
    gather(second_rows, odd)
    send(chunks - 2).start()
    finish(chunks - 1, odd)
    send(chunks - 1).start()

    fine_slots[...] = places(fine_lists[...], LEAVES, 0)
    coarse_slots[...] = places(coarse_lists[...], PARENTS, LEAVES)
    transfers.wait()
    low = low_half(RANK)
    low_points = low_half(POINTS)

    def put(n, block):
        skeleton[n] = block
        even_sent[n] = block

    for p in range(PARENTS):
        put(p, jnp.where(low, fine[2 * p], fine[2 * p + 1]))
    for q in range(PARENTS // 2):
        coarse = []
        for p in (2 * q, 2 * q + 1):
            pair = transfer_here[2 * p : 2 * p + 2].reshape(2 * RANK, RANK)
            stacked = fine[2 * p : 2 * p + 2].reshape(2 * RANK, 128)
            coarse.append(
                lax.dot_general(
                    pair, stacked, (((0,), (0,)), ((), ())), preferred_element_type=F32
                ).astype(BF16)
            )
        put(PARENTS + q, jnp.where(low, coarse[0], coarse[1]))
    odd_here = lax.rem(lax.axis_index("gy"), 2)
    last = (1 - odd_here) * (LEAVES - 2)
    edge = jnp.where(low_points, ordered_here[last], ordered_here[last + 1])
    even_sent[PAIRS:] = edge.reshape(EDGE, RANK, 128)
    last = odd_here * (LEAVES - 2)
    odd_edge[...] = jnp.where(low_points, ordered_here[last], ordered_here[last + 1])
    for chunk in range(ROWS // CHUNK):
        send(chunk).wait()


def order_points(points, perm, basis, transfer, fine_lists, coarse_lists):
    anywhere = pl.BlockSpec(memory_space=pl.ANY)
    vmem = pl.BlockSpec(memory_space=VMEM)
    return pl.pallas_call(
        order_kernel,
        out_shape=(
            jax.ShapeDtypeStruct((LEAVES, POINTS, 128), BF16),
            jax.ShapeDtypeStruct((PAIRS, RANK, 128), BF16),
            jax.ShapeDtypeStruct((PAIRS + EDGE, RANK, 128), BF16),
            jax.ShapeDtypeStruct((POINTS, 128), BF16),
            jax.ShapeDtypeStruct(fine_lists.shape, jnp.int32),
            jax.ShapeDtypeStruct(coarse_lists.shape, jnp.int32),
        ),
        in_specs=[anywhere] * 4 + [vmem] * 2,
        out_specs=(anywhere,) + (vmem,) * 5,
        scratch_shapes=[
            pltpu.VMEM((ROWS, 128), F32),
            pltpu.VMEM((CHUNK, 128), F32),
            pltpu.VMEM((CHUNK, 128), F32),
            pltpu.VMEM((LEAVES, RANK, 128), BF16),
            pltpu.SMEM((CHUNK,), jnp.int32),
            pltpu.SMEM((CHUNK,), jnp.int32),
            pltpu.VMEM((COLS, ROWS), BF16),
            pltpu.VMEM((LEAVES, RANK, POINTS), BF16),
            pltpu.VMEM((LEAVES, RANK, RANK), BF16),
            pltpu.VMEM((LEAVES, POINTS, 128), BF16),
            pltpu.SemaphoreType.DMA((POINT_PARTS + 4,)),
            pltpu.SemaphoreType.DMA((ROWS // CHUNK,)),
        ],
        compiler_params=params(ORDER_MIB),
        name="order_points",
    )(perm, points, basis, transfer, fine_lists, coarse_lists)


def turn_kernel(blocks, turned, table):
    half = RANK // 2
    targets = 128 // ENTRIES
    low = low_half(half)

    def tile(n, _):
        entries = pl.ds(pl.multiple_of(n * 128, 128), 128)
        for k in range(half):
            block = jnp.concatenate([blocks[k, :, entries], blocks[k + half, :, entries]], axis=0)
            table[pl.ds(k, 128, stride=PITCH), :] = block.astype(F32).T
        for t in range(targets):
            into = turned.at[n * targets + t]
            for j in range(0, ENTRIES, 2):
                first = table[pl.ds((t * ENTRIES + j) * PITCH, half), :]
                second = table[pl.ds((t * ENTRIES + j + 1) * PITCH, half), :]
                into[:half, j * 64 : (j + 2) * 64] = jnp.where(
                    low, first, pltpu.roll(second, 64, 1)
                ).astype(BF16)
                into[half:, j * 64 : (j + 2) * 64] = jnp.where(
                    low, pltpu.roll(first, 64, 1), second
                ).astype(BF16)
        return 0

    lax.fori_loop(0, blocks.shape[2] // 128, tile, 0)


def turn_blocks(blocks):
    return pl.pallas_call(
        turn_kernel,
        out_shape=jax.ShapeDtypeStruct((blocks.shape[2] // ENTRIES, RANK, ENTRIES * RANK), BF16),
        in_specs=[pl.BlockSpec(memory_space=VMEM)],
        out_specs=pl.BlockSpec(memory_space=VMEM),
        scratch_shapes=[pltpu.VMEM((128 * PITCH, 128), F32)],
        compiler_params=params(24),
        cost_estimate=pl.CostEstimate(
            flops=0, bytes_accessed=6 * blocks.size, transcendentals=0
        ),
        name="turn_blocks",
    )(blocks)


def near_kernel(
    targets, sources, count, even, odd, ordered, blocks, total, window, held, sem, sems
):
    steps = TASKS // TASK_STEP

    def fetch(step):
        slot = lax.rem(step, HELD)
        tasks = pl.ds(step * TASK_STEP, TASK_STEP)
        return pltpu.make_async_copy(blocks.at[tasks], held.at[slot], sems.at[slot])

    copy = pltpu.make_async_copy(ordered, window.at[pl.ds(HALO, LEAVES)], sem)
    copy.start()
    for step in range(HELD - 1):
        fetch(step).start()
    low = low_half(POINTS)
    odd_here = lax.rem(lax.axis_index("gy"), 2)
    from_even = even[PAIRS:].reshape(POINTS, 128)
    after = LEAVES + HALO
    for pair, place in ((from_even, (1 - odd_here) * after), (odd[...], odd_here * after)):
        swapped = swap_halves(pair)
        window[place] = jnp.where(low, pair, swapped)
        window[place + 1] = jnp.where(low, swapped, pair)
    total[...] = jnp.zeros_like(total)
    copy.wait()

    def one_step(step, _):
        slot = lax.rem(step, HELD)
        fetch(step).wait()

        @pl.when(step < steps - (HELD - 1))
        def _():
            fetch(step + HELD - 1).start()

        for i in range(TASK_STEP):
            task = step * TASK_STEP + i
            target = jnp.where(task < count[0], targets[task], LEAVES)
            total[target] += jnp.dot(
                held[slot, i], window[sources[task]], preferred_element_type=F32
            )
        return 0

    lax.fori_loop(0, steps, one_step, 0)


def near_field(targets, sources, count, even, odd, ordered, blocks):
    return pl.pallas_call(
        near_kernel,
        out_shape=jax.ShapeDtypeStruct((LEAVES + 1, POINTS, 128), F32),
        in_specs=[
            pl.BlockSpec(memory_space=SMEM),
            pl.BlockSpec(memory_space=SMEM),
            pl.BlockSpec(memory_space=SMEM),
            pl.BlockSpec(memory_space=VMEM),
            pl.BlockSpec(memory_space=VMEM),
            pl.BlockSpec(memory_space=pl.ANY),
            pl.BlockSpec(memory_space=pl.ANY),
        ],
        out_specs=pl.BlockSpec(memory_space=VMEM),
        scratch_shapes=[
            pltpu.VMEM((LEAVES + 2 * HALO, POINTS, 128), BF16),
            pltpu.VMEM((HELD, TASK_STEP, POINTS, POINTS), BF16),
            pltpu.SemaphoreType.DMA,
            pltpu.SemaphoreType.DMA((HELD,)),
        ],
        compiler_params=params(NEAR_MIB),
        cost_estimate=pl.CostEstimate(
            flops=2 * TASKS * POINTS * POINTS * 128,
            bytes_accessed=2 * TASKS * POINTS * POINTS,
            transcendentals=0,
        ),
        name="near_field",
    )(targets, sources, count, even, odd, ordered, blocks)


def result_kernel(*refs):
    perm, fine_slots, coarse_slots = refs[:3]
    own, y_even, y_odd, x_even, x_odd, xy_even, xy_odd = refs[3:10]
    fine, coarse, transfer, basis, near, out = refs[10:16]
    spread, below, above, first_rows, second_rows, table, wide = refs[16:23]
    first_places, second_places, sems, out_sems = refs[23:]
    skeletons = [(own, 0), (y_even, 0), (y_odd, 0), (x_even, 0), (xy_even, 0), (xy_odd, 0)]
    skeletons += [(x_odd, 0), (xy_even, PAIRS), (xy_odd, PAIRS)]
    steps = LEAVES // LEAF_STEP

    def load_places(step, into, sem):
        return pltpu.make_async_copy(perm.at[pl.ds(step * CHUNK, CHUNK)], into, sems.at[sem])

    load_places(0, first_places, 0).start()
    load_places(1, second_places, 1).start()
    low = low_half(RANK)
    keep = (low.astype(F32).astype(BF16), (~low).astype(F32).astype(BF16))
    for a, (source, start) in enumerate(skeletons):

        def part(p, _):
            for z in range(2):
                spread[a * 2 * PAIRS + 2 * p + z] = source[start + p] * keep[z]
            return 0

        lax.fori_loop(0, PAIRS, part, 0, unroll=8)

    def coupled(matrix, slots):
        picked = [spread[slot] for slot in slots]
        return jnp.dot(matrix, jnp.concatenate(picked, axis=0), preferred_element_type=F32)

    def couple(step, _):
        for p in range(2):
            parent = step * 2 + p
            above[parent] = coupled(
                coarse[parent], [coarse_slots[parent, j] for j in range(ENTRIES)]
            )
        for c in range(4):
            leaf = step * 4 + c
            below[leaf] = coupled(fine[leaf], [fine_slots[j, leaf] for j in range(ENTRIES)])
        return 0

    lax.fori_loop(0, LEAVES // 4, couple, 0)

    def fold(halves):
        return halves + pltpu.roll(halves, 64, 1)

    def compute(step, rows):
        for p in range(LEAF_STEP // 2):
            parent = step * (LEAF_STEP // 2) + p
            from_parent = fold(above[parent]).astype(BF16)
            for z in range(2):
                c = 2 * p + z
                leaf = step * LEAF_STEP + c
                local = fold(below[leaf])
                local += jnp.dot(transfer[leaf], from_parent, preferred_element_type=F32)
                far = lax.dot_general(
                    basis[leaf],
                    local.astype(BF16),
                    (((0,), (0,)), ((), ())),
                    preferred_element_type=F32,
                )
                rows[c * POINTS : (c + 1) * POINTS, :] = far + near[leaf]

    def scatter(places, rows):
        for i in range(CHUNK):
            table[pl.ds(places[i], 1), :] = rows[i : i + 1, :]

    compute(0, first_rows)

    def two_steps(pair, _):
        load_places(2 * pair, first_places, 0).wait()
        compute(2 * pair + 1, second_rows)
        scatter(first_places, first_rows)
        more = pair < steps // 2 - 1

        @pl.when(more)
        def _():
            load_places(2 * pair + 2, first_places, 0).start()

        load_places(2 * pair + 1, second_places, 1).wait()
        compute(jnp.minimum(2 * pair + 2, steps - 1), first_rows)
        scatter(second_places, second_rows)

        @pl.when(more)
        def _():
            load_places(2 * pair + 3, second_places, 1).start()

        return 0

    lax.fori_loop(0, steps // 2, two_steps, 0)

    low = low_half(128)
    sends = []
    for n in range(OUT_PARTS):
        width = ROWS // OUT_PARTS
        for c in range(n * width // 128, (n + 1) * width // 128):
            block = table[c * 128 : (c + 1) * 128, :]
            high = block.astype(BF16)
            rest = (block - high.astype(F32)).astype(BF16)
            both = jnp.where(low, high, rest).T.astype(F32)
            wide[:, c * 128 : (c + 1) * 128] = both[:COLS] + both[COLS:]
        span = pl.ds(n * width, width)
        sends.append(pltpu.make_async_copy(wide.at[:, span], out.at[:, span], out_sems.at[n]))
        sends[-1].start()
    for send in sends:
        send.wait()


def result(perm, fine_slots, coarse_slots, skeletons, fine, coarse, transfer, basis, near):
    return pl.pallas_call(
        result_kernel,
        out_shape=jax.ShapeDtypeStruct((COLS, ROWS), F32),
        in_specs=[
            pl.BlockSpec(memory_space=pl.ANY),
            *[pl.BlockSpec(memory_space=SMEM)] * 2,
            *[pl.BlockSpec(memory_space=VMEM)] * 12,
        ],
        out_specs=pl.BlockSpec(memory_space=pl.ANY),
        scratch_shapes=[
            pltpu.VMEM((9 * 2 * PAIRS, RANK, 128), BF16),
            pltpu.VMEM((LEAVES, RANK, 128), F32),
            pltpu.VMEM((PARENTS, RANK, 128), F32),
            pltpu.VMEM((CHUNK, 128), F32),
            pltpu.VMEM((CHUNK, 128), F32),
            pltpu.VMEM((ROWS, 128), F32),
            pltpu.VMEM((COLS, ROWS), F32),
            pltpu.SMEM((CHUNK,), jnp.int32),
            pltpu.SMEM((CHUNK,), jnp.int32),
            pltpu.SemaphoreType.DMA((2,)),
            pltpu.SemaphoreType.DMA((OUT_PARTS,)),
        ],
        compiler_params=params(36),
        name="result",
    )(perm, fine_slots, coarse_slots, *skeletons, fine, coarse, transfer, basis, near)


def swaps(count, odd):
    pairs = [((i + odd) % count, (i + odd + 1) % count) for i in range(0, count, 2)]
    return [(a, b) for a, b in pairs] + [(b, a) for a, b in pairs]


def swap(x, axis, odd):
    return lax.ppermute(x, axis, swaps(lax.axis_size(axis), odd))


def on_device(
    points_in,
    tree_perm,
    basis,
    transfer,
    couple_fine,
    couple_coarse,
    list_fine,
    list_coarse,
    near_blocks,
    near_target,
    near_source,
    task_count,
):
    basis_rows = basis.transpose(0, 2, 1)
    ordered, own, even_sent, odd_edge, fine_slots, coarse_slots = order_points(
        points_in.T, tree_perm, basis_rows, transfer, list_fine.T, list_coarse
    )
    x_even = swap(own, "gx", 0)
    x_odd = swap(own, "gx", 1)
    y_even = swap(even_sent, "gy", 0)
    y_odd = swap(own, "gy", 1)
    both = ("gx", "gy")
    line = [(i, i + 1) for i in range(1, lax.axis_size(both) - 1, 2)]
    odd_edge = lax.ppermute(odd_edge, both, line + [(b, a) for a, b in line])
    fine = turn_blocks(couple_fine.transpose(1, 2, 0))
    coarse = turn_blocks(couple_coarse.transpose(1, 2, 0))
    near = near_field(near_target, near_source, task_count, y_even, odd_edge, ordered, near_blocks)
    x_both = jnp.concatenate([x_even, x_odd], axis=0)
    xy_even = swap(x_both, "gy", 0)
    xy_odd = swap(x_both, "gy", 1)
    skeletons = (own, y_even, y_odd, x_even, x_odd, xy_even, xy_odd)
    out = result(
        tree_perm, fine_slots, coarse_slots, skeletons, fine, coarse, transfer, basis_rows, near
    )
    return out.T


def solution(mesh):
    flat = P(("gx", "gy"))
    return jax.shard_map(
        on_device,
        mesh=mesh,
        in_specs=(flat,) * 12,
        out_specs=flat,
        check_vma=False,
    )
```

```python
import jax
import jax.numpy as jnp
from jax import lax
from jax.experimental import pallas as pl
from jax.experimental.pallas import tpu as pltpu
from jax.sharding import PartitionSpec as P

LEAVES = 32
PARENTS = LEAVES // 2
POINTS = 256
RANK = 64
COLS = 64
ENTRIES = 16
HALO = 2
TASKS = 128
ROWS = LEAVES * POINTS
PAIRS = LEAVES // 2 + PARENTS // 2
EDGE = POINTS // RANK
TASK_STEP = 16
LEAF_STEP = 4
CHUNK = 1024
POINT_PARTS = 4
OUT_PARTS = 8
ORDER_MIB = 60
NEAR_MIB = 36
HELD = 4
PITCH = RANK // 2 + 1

SMEM = pltpu.SMEM
VMEM = pltpu.VMEM
F32 = jnp.float32
BF16 = jnp.bfloat16


def params(mib):
    return pltpu.CompilerParams(vmem_limit_bytes=mib << 20)


def low_half(rows):
    return lax.broadcasted_iota(jnp.int32, (rows, 128), 1) < 64


def swap_halves(x):
    return jnp.concatenate([x[:, 64:], x[:, :64]], axis=1)


def places(lists, clusters, first):
    outer, inner = lax.axis_size("gx"), lax.axis_size("gy")
    gx, gy = lax.axis_index("gx"), lax.axis_index("gy")
    owner = lists >> (clusters.bit_length() - 1)
    step_x = ((owner >> (inner.bit_length() - 1)) - gx) & (outer - 1)
    step_y = (owner - gy) & (inner - 1)
    swap_x = jnp.where(step_x == 1, 1 + (gx & 1), 2 - (gx & 1))
    swap_y = jnp.where(step_y == 1, 1 + (gy & 1), 2 - (gy & 1))
    array = jnp.where(step_x == 0, 0, swap_x) * 3 + jnp.where(step_y == 0, 0, swap_y)
    return array * (2 * PAIRS) + first + (lists & (clusters - 1))


def order_kernel(
    perm,
    points,
    basis,
    transfer,
    fine_lists,
    coarse_lists,
    ordered,
    skeleton,
    even_sent,
    odd_edge,
    fine_slots,
    coarse_slots,
    table,
    even,
    odd,
    fine,
    first_rows,
    second_rows,
    points_here,
    basis_here,
    transfer_here,
    ordered_here,
    sems,
    out_sems,
):
    width = ROWS // POINT_PARTS

    def part(n):
        span = pl.ds(n * width, width)
        return pltpu.make_async_copy(points.at[:, span], points_here.at[:, span], sems.at[n])

    def load_rows(chunk, into, sem):
        return pltpu.make_async_copy(
            perm.at[pl.ds(chunk * CHUNK, CHUNK)], into, sems.at[POINT_PARTS + sem]
        )

    for n in range(POINT_PARTS):
        part(n).start()
    load_rows(0, first_rows, 0).start()
    load_rows(1, second_rows, 1).start()
    bases = pltpu.make_async_copy(basis, basis_here, sems.at[POINT_PARTS + 2])
    transfers = pltpu.make_async_copy(transfer, transfer_here, sems.at[POINT_PARTS + 3])
    bases.start()
    transfers.start()
    for n in range(POINT_PARTS):
        part(n).wait()
        for c in range(n * width // 128, (n + 1) * width // 128):
            block = points_here[:, c * 128 : (c + 1) * 128].astype(F32)
            table[c * 128 : (c + 1) * 128, :] = jnp.concatenate([block, block], axis=0).T
    bases.wait()

    leaves = CHUNK // POINTS

    def gather(places, into):
        for i in range(CHUNK):
            into[i : i + 1, :] = table[pl.ds(places[i], 1), :]

    def finish(chunk, source):
        for n in range(leaves):
            leaf = chunk * leaves + n
            block = source[n * POINTS : (n + 1) * POINTS, :].astype(BF16)
            ordered_here[leaf] = block
            fine[leaf] = jnp.dot(basis_here[leaf], block, preferred_element_type=F32).astype(BF16)

    def send(chunk):
        span = pl.ds(chunk * leaves, leaves)
        return pltpu.make_async_copy(ordered_here.at[span], ordered.at[span], out_sems.at[chunk])

    chunks = ROWS // CHUNK
    load_rows(0, first_rows, 0).wait()
    gather(first_rows, even)

    def two_chunks(step, _):
        load_rows(2 * step + 1, second_rows, 1).wait()
        load_rows(2 * step + 2, first_rows, 0).start()
        finish(2 * step, even)
        gather(second_rows, odd)
        send(2 * step).start()

        load_rows(2 * step + 3, second_rows, 1).start()
        load_rows(2 * step + 2, first_rows, 0).wait()
        finish(2 * step + 1, odd)
        gather(first_rows, even)
        send(2 * step + 1).start()
        return 0

    lax.fori_loop(0, chunks // 2 - 1, two_chunks, 0)
    load_rows(chunks - 1, second_rows, 1).wait()
    finish(chunks - 2, even)
    gather(second_rows, odd)
    send(chunks - 2).start()
    finish(chunks - 1, odd)
    send(chunks - 1).start()

    fine_slots[...] = places(fine_lists[...], LEAVES, 0)
    coarse_slots[...] = places(coarse_lists[...], PARENTS, LEAVES)
    transfers.wait()
    low = low_half(RANK)
    low_points = low_half(POINTS)

    def put(n, block):
        skeleton[n] = block
        even_sent[n] = block

    for p in range(PARENTS):
        put(p, jnp.where(low, fine[2 * p], fine[2 * p + 1]))
    for q in range(PARENTS // 2):
        coarse = []
        for p in (2 * q, 2 * q + 1):
            pair = transfer_here[2 * p : 2 * p + 2].reshape(2 * RANK, RANK)
            stacked = fine[2 * p : 2 * p + 2].reshape(2 * RANK, 128)
            coarse.append(
                lax.dot_general(
                    pair, stacked, (((0,), (0,)), ((), ())), preferred_element_type=F32
                ).astype(BF16)
            )
        put(PARENTS + q, jnp.where(low, coarse[0], coarse[1]))
    odd_here = lax.rem(lax.axis_index("gy"), 2)
    last = (1 - odd_here) * (LEAVES - 2)
    edge = jnp.where(low_points, ordered_here[last], ordered_here[last + 1])
    even_sent[PAIRS:] = edge.reshape(EDGE, RANK, 128)
    last = odd_here * (LEAVES - 2)
    odd_edge[...] = jnp.where(low_points, ordered_here[last], ordered_here[last + 1])
    for chunk in range(ROWS // CHUNK):
        send(chunk).wait()


def order_points(points, perm, basis, transfer, fine_lists, coarse_lists):
    anywhere = pl.BlockSpec(memory_space=pl.ANY)
    vmem = pl.BlockSpec(memory_space=VMEM)
    return pl.pallas_call(
        order_kernel,
        out_shape=(
            jax.ShapeDtypeStruct((LEAVES, POINTS, 128), BF16),
            jax.ShapeDtypeStruct((PAIRS, RANK, 128), BF16),
            jax.ShapeDtypeStruct((PAIRS + EDGE, RANK, 128), BF16),
            jax.ShapeDtypeStruct((POINTS, 128), BF16),
            jax.ShapeDtypeStruct(fine_lists.shape, jnp.int32),
            jax.ShapeDtypeStruct(coarse_lists.shape, jnp.int32),
        ),
        in_specs=[anywhere] * 4 + [vmem] * 2,
        out_specs=(anywhere,) + (vmem,) * 5,
        scratch_shapes=[
            pltpu.VMEM((ROWS, 128), F32),
            pltpu.VMEM((CHUNK, 128), F32),
            pltpu.VMEM((CHUNK, 128), F32),
            pltpu.VMEM((LEAVES, RANK, 128), BF16),
            pltpu.SMEM((CHUNK,), jnp.int32),
            pltpu.SMEM((CHUNK,), jnp.int32),
            pltpu.VMEM((COLS, ROWS), BF16),
            pltpu.VMEM((LEAVES, RANK, POINTS), BF16),
            pltpu.VMEM((LEAVES, RANK, RANK), BF16),
            pltpu.VMEM((LEAVES, POINTS, 128), BF16),
            pltpu.SemaphoreType.DMA((POINT_PARTS + 4,)),
            pltpu.SemaphoreType.DMA((ROWS // CHUNK,)),
        ],
        compiler_params=params(ORDER_MIB),
        name="order_points",
    )(perm, points, basis, transfer, fine_lists, coarse_lists)


def turn_kernel(blocks, turned, table):
    half = RANK // 2
    targets = 128 // ENTRIES
    low = low_half(half)

    def tile(n, _):
        entries = pl.ds(pl.multiple_of(n * 128, 128), 128)
        for k in range(half):
            block = jnp.concatenate([blocks[k, :, entries], blocks[k + half, :, entries]], axis=0)
            table[pl.ds(k, 128, stride=PITCH), :] = block.astype(F32).T
        for t in range(targets):
            into = turned.at[n * targets + t]
            for j in range(0, ENTRIES, 2):
                first = table[pl.ds((t * ENTRIES + j) * PITCH, half), :]
                second = table[pl.ds((t * ENTRIES + j + 1) * PITCH, half), :]
                into[:half, j * 64 : (j + 2) * 64] = jnp.where(
                    low, first, pltpu.roll(second, 64, 1)
                ).astype(BF16)
                into[half:, j * 64 : (j + 2) * 64] = jnp.where(
                    low, pltpu.roll(first, 64, 1), second
                ).astype(BF16)
        return 0

    lax.fori_loop(0, blocks.shape[2] // 128, tile, 0)


def turn_blocks(blocks):
    return pl.pallas_call(
        turn_kernel,
        out_shape=jax.ShapeDtypeStruct((blocks.shape[2] // ENTRIES, RANK, ENTRIES * RANK), BF16),
        in_specs=[pl.BlockSpec(memory_space=VMEM)],
        out_specs=pl.BlockSpec(memory_space=VMEM),
        scratch_shapes=[pltpu.VMEM((128 * PITCH, 128), F32)],
        compiler_params=params(24),
        cost_estimate=pl.CostEstimate(
            flops=0, bytes_accessed=6 * blocks.size, transcendentals=0
        ),
        name="turn_blocks",
    )(blocks)


def near_kernel(
    targets, sources, count, even, odd, ordered, blocks, total, window, held, sem, sems
):
    steps = TASKS // TASK_STEP

    def fetch(step):
        slot = lax.rem(step, HELD)
        tasks = pl.ds(step * TASK_STEP, TASK_STEP)
        return pltpu.make_async_copy(blocks.at[tasks], held.at[slot], sems.at[slot])

    copy = pltpu.make_async_copy(ordered, window.at[pl.ds(HALO, LEAVES)], sem)
    copy.start()
    for step in range(HELD - 1):
        fetch(step).start()
    low = low_half(POINTS)
    odd_here = lax.rem(lax.axis_index("gy"), 2)
    from_even = even[PAIRS:].reshape(POINTS, 128)
    after = LEAVES + HALO
    for pair, place in ((from_even, (1 - odd_here) * after), (odd[...], odd_here * after)):
        swapped = swap_halves(pair)
        window[place] = jnp.where(low, pair, swapped)
        window[place + 1] = jnp.where(low, swapped, pair)
    total[...] = jnp.zeros_like(total)
    copy.wait()

    def one_step(step, _):
        slot = lax.rem(step, HELD)
        fetch(step).wait()

        @pl.when(step < steps - (HELD - 1))
        def _():
            fetch(step + HELD - 1).start()

        for i in range(TASK_STEP):
            task = step * TASK_STEP + i
            target = jnp.where(task < count[0], targets[task], LEAVES)
            total[target] += jnp.dot(
                held[slot, i], window[sources[task]], preferred_element_type=F32
            )
        return 0

    lax.fori_loop(0, steps, one_step, 0)


def near_field(targets, sources, count, even, odd, ordered, blocks):
    return pl.pallas_call(
        near_kernel,
        out_shape=jax.ShapeDtypeStruct((LEAVES + 1, POINTS, 128), F32),
        in_specs=[
            pl.BlockSpec(memory_space=SMEM),
            pl.BlockSpec(memory_space=SMEM),
            pl.BlockSpec(memory_space=SMEM),
            pl.BlockSpec(memory_space=VMEM),
            pl.BlockSpec(memory_space=VMEM),
            pl.BlockSpec(memory_space=pl.ANY),
            pl.BlockSpec(memory_space=pl.ANY),
        ],
        out_specs=pl.BlockSpec(memory_space=VMEM),
        scratch_shapes=[
            pltpu.VMEM((LEAVES + 2 * HALO, POINTS, 128), BF16),
            pltpu.VMEM((HELD, TASK_STEP, POINTS, POINTS), BF16),
            pltpu.SemaphoreType.DMA,
            pltpu.SemaphoreType.DMA((HELD,)),
        ],
        compiler_params=params(NEAR_MIB),
        cost_estimate=pl.CostEstimate(
            flops=2 * TASKS * POINTS * POINTS * 128,
            bytes_accessed=2 * TASKS * POINTS * POINTS,
            transcendentals=0,
        ),
        name="near_field",
    )(targets, sources, count, even, odd, ordered, blocks)


def result_kernel(*refs):
    perm, fine_slots, coarse_slots = refs[:3]
    own, y_even, y_odd, x_even, x_odd, xy_even, xy_odd = refs[3:10]
    fine, coarse, transfer, basis, near, out = refs[10:16]
    spread, below, above, first_rows, second_rows, table, wide = refs[16:23]
    first_places, second_places, sems, out_sems = refs[23:]
    skeletons = [(own, 0), (y_even, 0), (y_odd, 0), (x_even, 0), (xy_even, 0), (xy_odd, 0)]
    skeletons += [(x_odd, 0), (xy_even, PAIRS), (xy_odd, PAIRS)]
    steps = LEAVES // LEAF_STEP

    def load_places(step, into, sem):
        return pltpu.make_async_copy(perm.at[pl.ds(step * CHUNK, CHUNK)], into, sems.at[sem])

    load_places(0, first_places, 0).start()
    load_places(1, second_places, 1).start()
    low = low_half(RANK)
    keep = (low.astype(F32).astype(BF16), (~low).astype(F32).astype(BF16))
    for a, (source, start) in enumerate(skeletons):

        def part(p, _):
            for z in range(2):
                spread[a * 2 * PAIRS + 2 * p + z] = source[start + p] * keep[z]
            return 0

        lax.fori_loop(0, PAIRS, part, 0, unroll=8)

    def coupled(matrix, slots):
        picked = [spread[slot] for slot in slots]
        return jnp.dot(matrix, jnp.concatenate(picked, axis=0), preferred_element_type=F32)

    def couple(step, _):
        for p in range(2):
            parent = step * 2 + p
            above[parent] = coupled(
                coarse[parent], [coarse_slots[parent, j] for j in range(ENTRIES)]
            )
        for c in range(4):
            leaf = step * 4 + c
            below[leaf] = coupled(fine[leaf], [fine_slots[j, leaf] for j in range(ENTRIES)])
        return 0

    lax.fori_loop(0, LEAVES // 4, couple, 0)

    def fold(halves):
        return halves + pltpu.roll(halves, 64, 1)

    def compute(step, rows):
        for p in range(LEAF_STEP // 2):
            parent = step * (LEAF_STEP // 2) + p
            from_parent = fold(above[parent]).astype(BF16)
            for z in range(2):
                c = 2 * p + z
                leaf = step * LEAF_STEP + c
                local = fold(below[leaf])
                local += jnp.dot(transfer[leaf], from_parent, preferred_element_type=F32)
                far = lax.dot_general(
                    basis[leaf],
                    local.astype(BF16),
                    (((0,), (0,)), ((), ())),
                    preferred_element_type=F32,
                )
                rows[c * POINTS : (c + 1) * POINTS, :] = far + near[leaf]

    def scatter(places, rows):
        for i in range(CHUNK):
            table[pl.ds(places[i], 1), :] = rows[i : i + 1, :]

    compute(0, first_rows)

    def two_steps(pair, _):
        load_places(2 * pair, first_places, 0).wait()
        compute(2 * pair + 1, second_rows)
        scatter(first_places, first_rows)
        more = pair < steps // 2 - 1

        @pl.when(more)
        def _():
            load_places(2 * pair + 2, first_places, 0).start()

        load_places(2 * pair + 1, second_places, 1).wait()
        compute(jnp.minimum(2 * pair + 2, steps - 1), first_rows)
        scatter(second_places, second_rows)

        @pl.when(more)
        def _():
            load_places(2 * pair + 3, second_places, 1).start()

        return 0

    lax.fori_loop(0, steps // 2, two_steps, 0)

    low = low_half(128)
    sends = []
    for n in range(OUT_PARTS):
        width = ROWS // OUT_PARTS
        for c in range(n * width // 128, (n + 1) * width // 128):
            block = table[c * 128 : (c + 1) * 128, :]
            high = block.astype(BF16)
            rest = (block - high.astype(F32)).astype(BF16)
            both = jnp.where(low, high, rest).T.astype(F32)
            wide[:, c * 128 : (c + 1) * 128] = both[:COLS] + both[COLS:]
        span = pl.ds(n * width, width)
        sends.append(pltpu.make_async_copy(wide.at[:, span], out.at[:, span], out_sems.at[n]))
        sends[-1].start()
    for send in sends:
        send.wait()


def result(perm, fine_slots, coarse_slots, skeletons, fine, coarse, transfer, basis, near):
    return pl.pallas_call(
        result_kernel,
        out_shape=jax.ShapeDtypeStruct((COLS, ROWS), F32),
        in_specs=[
            pl.BlockSpec(memory_space=pl.ANY),
            *[pl.BlockSpec(memory_space=SMEM)] * 2,
            *[pl.BlockSpec(memory_space=VMEM)] * 12,
        ],
        out_specs=pl.BlockSpec(memory_space=pl.ANY),
        scratch_shapes=[
            pltpu.VMEM((9 * 2 * PAIRS, RANK, 128), BF16),
            pltpu.VMEM((LEAVES, RANK, 128), F32),
            pltpu.VMEM((PARENTS, RANK, 128), F32),
            pltpu.VMEM((CHUNK, 128), F32),
            pltpu.VMEM((CHUNK, 128), F32),
            pltpu.VMEM((ROWS, 128), F32),
            pltpu.VMEM((COLS, ROWS), F32),
            pltpu.SMEM((CHUNK,), jnp.int32),
            pltpu.SMEM((CHUNK,), jnp.int32),
            pltpu.SemaphoreType.DMA((2,)),
            pltpu.SemaphoreType.DMA((OUT_PARTS,)),
        ],
        compiler_params=params(36),
        name="result",
    )(perm, fine_slots, coarse_slots, *skeletons, fine, coarse, transfer, basis, near)


def join_kernel(first, second, *refs):
    joined, sems = refs[-2:]
    copies = [
        pltpu.make_async_copy(x, joined.at[pl.ds(n * PAIRS, PAIRS)], sems.at[n])
        for n, x in enumerate((first, second))
    ]
    for copy in copies:
        copy.start()
    for copy in copies:
        copy.wait()


def join(first, second, *earlier):
    anywhere = pl.BlockSpec(memory_space=pl.ANY)
    return pl.pallas_call(
        join_kernel,
        out_shape=jax.ShapeDtypeStruct((2 * PAIRS, RANK, 128), BF16),
        in_specs=[anywhere] * (2 + len(earlier)),
        out_specs=anywhere,
        scratch_shapes=[pltpu.SemaphoreType.DMA((2,))],
        compiler_params=params(1),
        name="join",
    )(first, second, *earlier)


def swaps(count, odd):
    pairs = [((i + odd) % count, (i + odd + 1) % count) for i in range(0, count, 2)]
    return [(a, b) for a, b in pairs] + [(b, a) for a, b in pairs]


def swap(x, axis, odd):
    return lax.ppermute(x, axis, swaps(lax.axis_size(axis), odd))


def on_device(
    points_in,
    tree_perm,
    basis,
    transfer,
    couple_fine,
    couple_coarse,
    list_fine,
    list_coarse,
    near_blocks,
    near_target,
    near_source,
    task_count,
):
    basis_rows = basis.transpose(0, 2, 1)
    ordered, own, even_sent, odd_edge, fine_slots, coarse_slots = order_points(
        points_in.T, tree_perm, basis_rows, transfer, list_fine.T, list_coarse
    )
    x_even = swap(own, "gx", 0)
    x_odd = swap(own, "gx", 1)
    y_even = swap(even_sent, "gy", 0)
    y_odd = swap(own, "gy", 1)
    both = ("gx", "gy")
    line = [(i, i + 1) for i in range(1, lax.axis_size(both) - 1, 2)]
    odd_edge = lax.ppermute(odd_edge, both, line + [(b, a) for a, b in line])
    fine = turn_blocks(couple_fine.transpose(1, 2, 0))
    coarse = turn_blocks(couple_coarse.transpose(1, 2, 0))
    near = near_field(near_target, near_source, task_count, y_even, odd_edge, ordered, near_blocks)
    x_both = join(x_even, x_odd, y_even, y_odd, odd_edge, fine, coarse)
    xy_even = swap(x_both, "gy", 0)
    xy_odd = swap(x_both, "gy", 1)
    skeletons = (own, y_even, y_odd, x_even, x_odd, xy_even, xy_odd)
    out = result(
        tree_perm, fine_slots, coarse_slots, skeletons, fine, coarse, transfer, basis_rows, near
    )
    return out.T


def solution(mesh):
    flat = P(("gx", "gy"))
    return jax.shard_map(
        on_device,
        mesh=mesh,
        in_specs=(flat,) * 12,
        out_specs=flat,
        check_vma=False,
    )
```

```python
import jax
import jax.numpy as jnp
from jax import lax
from jax.experimental import pallas as pl
from jax.experimental.pallas import tpu as pltpu
from jax.sharding import PartitionSpec as P

LEAVES = 32
PARENTS = LEAVES // 2
POINTS = 256
RANK = 64
COLS = 64
ENTRIES = 16
HALO = 2
TASKS = 128
ROWS = LEAVES * POINTS
PAIRS = LEAVES // 2 + PARENTS // 2
TASK_STEP = 16
LEAF_STEP = 4
CHUNK = 1024
POINT_PARTS = 4
OUT_PARTS = 8
ORDER_MIB = 60
NEAR_MIB = 36
HELD = 4
PITCH = RANK // 2 + 1

SMEM = pltpu.SMEM
VMEM = pltpu.VMEM
F32 = jnp.float32
BF16 = jnp.bfloat16


def params(mib):
    return pltpu.CompilerParams(vmem_limit_bytes=mib << 20)


def low_half(rows):
    return lax.broadcasted_iota(jnp.int32, (rows, 128), 1) < 64


def swap_halves(x):
    return jnp.concatenate([x[:, 64:], x[:, :64]], axis=1)


def places(lists, clusters, first):
    outer, inner = lax.axis_size("gx"), lax.axis_size("gy")
    gx, gy = lax.axis_index("gx"), lax.axis_index("gy")
    owner = lists >> (clusters.bit_length() - 1)
    step_x = ((owner >> (inner.bit_length() - 1)) - gx) & (outer - 1)
    step_y = (owner - gy) & (inner - 1)
    swap_x = jnp.where(step_x == 1, 1 + (gx & 1), 2 - (gx & 1))
    swap_y = jnp.where(step_y == 1, 1 + (gy & 1), 2 - (gy & 1))
    array = jnp.where(step_x == 0, 0, swap_x) * 3 + jnp.where(step_y == 0, 0, swap_y)
    return array * (2 * PAIRS) + first + (lists & (clusters - 1))


def order_kernel(
    perm,
    points,
    basis,
    transfer,
    fine_lists,
    coarse_lists,
    ordered,
    skeleton,
    even_edge,
    odd_edge,
    fine_slots,
    coarse_slots,
    table,
    even,
    odd,
    fine,
    first_rows,
    second_rows,
    points_here,
    basis_here,
    transfer_here,
    ordered_here,
    sems,
    out_sems,
):
    width = ROWS // POINT_PARTS

    def part(n):
        span = pl.ds(n * width, width)
        return pltpu.make_async_copy(points.at[:, span], points_here.at[:, span], sems.at[n])

    def load_rows(chunk, into, sem):
        return pltpu.make_async_copy(
            perm.at[pl.ds(chunk * CHUNK, CHUNK)], into, sems.at[POINT_PARTS + sem]
        )

    for n in range(POINT_PARTS):
        part(n).start()
    load_rows(0, first_rows, 0).start()
    load_rows(1, second_rows, 1).start()
    bases = pltpu.make_async_copy(basis, basis_here, sems.at[POINT_PARTS + 2])
    transfers = pltpu.make_async_copy(transfer, transfer_here, sems.at[POINT_PARTS + 3])
    bases.start()
    transfers.start()
    for n in range(POINT_PARTS):
        part(n).wait()
        for c in range(n * width // 128, (n + 1) * width // 128):
            block = points_here[:, c * 128 : (c + 1) * 128].astype(F32)
            table[c * 128 : (c + 1) * 128, :] = jnp.concatenate([block, block], axis=0).T
    bases.wait()

    leaves = CHUNK // POINTS

    def gather(places, into):
        for i in range(CHUNK):
            into[i : i + 1, :] = table[pl.ds(places[i], 1), :]

    def finish(chunk, source):
        for n in range(leaves):
            leaf = chunk * leaves + n
            block = source[n * POINTS : (n + 1) * POINTS, :].astype(BF16)
            ordered_here[leaf] = block
            fine[leaf] = jnp.dot(basis_here[leaf], block, preferred_element_type=F32).astype(BF16)

    def send(chunk):
        span = pl.ds(chunk * leaves, leaves)
        return pltpu.make_async_copy(ordered_here.at[span], ordered.at[span], out_sems.at[chunk])

    chunks = ROWS // CHUNK
    load_rows(0, first_rows, 0).wait()
    gather(first_rows, even)

    def two_chunks(step, _):
        load_rows(2 * step + 1, second_rows, 1).wait()
        load_rows(2 * step + 2, first_rows, 0).start()
        finish(2 * step, even)
        gather(second_rows, odd)
        send(2 * step).start()

        load_rows(2 * step + 3, second_rows, 1).start()
        load_rows(2 * step + 2, first_rows, 0).wait()
        finish(2 * step + 1, odd)
        gather(first_rows, even)
        send(2 * step + 1).start()
        return 0

    lax.fori_loop(0, chunks // 2 - 1, two_chunks, 0)
    load_rows(chunks - 1, second_rows, 1).wait()
    finish(chunks - 2, even)
    gather(second_rows, odd)
    send(chunks - 2).start()
    finish(chunks - 1, odd)
    send(chunks - 1).start()

    fine_slots[...] = places(fine_lists[...], LEAVES, 0)
    coarse_slots[...] = places(coarse_lists[...], PARENTS, LEAVES)
    transfers.wait()
    low = low_half(RANK)
    low_points = low_half(POINTS)

    for p in range(PARENTS):
        skeleton[p] = jnp.where(low, fine[2 * p], fine[2 * p + 1])
    for q in range(PARENTS // 2):
        coarse = []
        for p in (2 * q, 2 * q + 1):
            pair = transfer_here[2 * p : 2 * p + 2].reshape(2 * RANK, RANK)
            stacked = fine[2 * p : 2 * p + 2].reshape(2 * RANK, 128)
            coarse.append(
                lax.dot_general(
                    pair, stacked, (((0,), (0,)), ((), ())), preferred_element_type=F32
                ).astype(BF16)
            )
        skeleton[PARENTS + q] = jnp.where(low, coarse[0], coarse[1])
    odd_here = lax.rem(lax.axis_index("gy"), 2)
    last = (1 - odd_here) * (LEAVES - 2)
    even_edge[...] = jnp.where(low_points, ordered_here[last], ordered_here[last + 1])
    last = odd_here * (LEAVES - 2)
    odd_edge[...] = jnp.where(low_points, ordered_here[last], ordered_here[last + 1])
    for chunk in range(ROWS // CHUNK):
        send(chunk).wait()


def order_points(points, perm, basis, transfer, fine_lists, coarse_lists):
    anywhere = pl.BlockSpec(memory_space=pl.ANY)
    vmem = pl.BlockSpec(memory_space=VMEM)
    return pl.pallas_call(
        order_kernel,
        out_shape=(
            jax.ShapeDtypeStruct((LEAVES, POINTS, 128), BF16),
            jax.ShapeDtypeStruct((PAIRS, RANK, 128), BF16),
            jax.ShapeDtypeStruct((POINTS, 128), BF16),
            jax.ShapeDtypeStruct((POINTS, 128), BF16),
            jax.ShapeDtypeStruct(fine_lists.shape, jnp.int32),
            jax.ShapeDtypeStruct(coarse_lists.shape, jnp.int32),
        ),
        in_specs=[anywhere] * 4 + [vmem] * 2,
        out_specs=(anywhere,) + (vmem,) * 5,
        scratch_shapes=[
            pltpu.VMEM((ROWS, 128), F32),
            pltpu.VMEM((CHUNK, 128), F32),
            pltpu.VMEM((CHUNK, 128), F32),
            pltpu.VMEM((LEAVES, RANK, 128), BF16),
            pltpu.SMEM((CHUNK,), jnp.int32),
            pltpu.SMEM((CHUNK,), jnp.int32),
            pltpu.VMEM((COLS, ROWS), BF16),
            pltpu.VMEM((LEAVES, RANK, POINTS), BF16),
            pltpu.VMEM((LEAVES, RANK, RANK), BF16),
            pltpu.VMEM((LEAVES, POINTS, 128), BF16),
            pltpu.SemaphoreType.DMA((POINT_PARTS + 4,)),
            pltpu.SemaphoreType.DMA((ROWS // CHUNK,)),
        ],
        compiler_params=params(ORDER_MIB),
        name="order_points",
    )(perm, points, basis, transfer, fine_lists, coarse_lists)


def turn_kernel(blocks, turned, table):
    half = RANK // 2
    targets = 128 // ENTRIES
    low = low_half(half)

    def tile(n, _):
        entries = pl.ds(pl.multiple_of(n * 128, 128), 128)
        for k in range(half):
            block = jnp.concatenate([blocks[k, :, entries], blocks[k + half, :, entries]], axis=0)
            table[pl.ds(k, 128, stride=PITCH), :] = block.astype(F32).T
        for t in range(targets):
            into = turned.at[n * targets + t]
            for j in range(0, ENTRIES, 2):
                first = table[pl.ds((t * ENTRIES + j) * PITCH, half), :]
                second = table[pl.ds((t * ENTRIES + j + 1) * PITCH, half), :]
                into[:half, j * 64 : (j + 2) * 64] = jnp.where(
                    low, first, pltpu.roll(second, 64, 1)
                ).astype(BF16)
                into[half:, j * 64 : (j + 2) * 64] = jnp.where(
                    low, pltpu.roll(first, 64, 1), second
                ).astype(BF16)
        return 0

    lax.fori_loop(0, blocks.shape[2] // 128, tile, 0)


def turn_blocks(blocks):
    return pl.pallas_call(
        turn_kernel,
        out_shape=jax.ShapeDtypeStruct((blocks.shape[2] // ENTRIES, RANK, ENTRIES * RANK), BF16),
        in_specs=[pl.BlockSpec(memory_space=VMEM)],
        out_specs=pl.BlockSpec(memory_space=VMEM),
        scratch_shapes=[pltpu.VMEM((128 * PITCH, 128), F32)],
        compiler_params=params(24),
        cost_estimate=pl.CostEstimate(
            flops=0, bytes_accessed=6 * blocks.size, transcendentals=0
        ),
        name="turn_blocks",
    )(blocks)


def near_kernel(
    targets, sources, count, even, odd, ordered, blocks, total, window, held, sem, sems
):
    steps = TASKS // TASK_STEP

    def fetch(step):
        slot = lax.rem(step, HELD)
        tasks = pl.ds(step * TASK_STEP, TASK_STEP)
        return pltpu.make_async_copy(blocks.at[tasks], held.at[slot], sems.at[slot])

    copy = pltpu.make_async_copy(ordered, window.at[pl.ds(HALO, LEAVES)], sem)
    copy.start()
    for step in range(HELD - 1):
        fetch(step).start()
    low = low_half(POINTS)
    odd_here = lax.rem(lax.axis_index("gy"), 2)
    after = LEAVES + HALO
    for pair, place in ((even[...], (1 - odd_here) * after), (odd[...], odd_here * after)):
        swapped = swap_halves(pair)
        window[place] = jnp.where(low, pair, swapped)
        window[place + 1] = jnp.where(low, swapped, pair)
    total[...] = jnp.zeros_like(total)
    copy.wait()

    def one_step(step, _):
        slot = lax.rem(step, HELD)
        fetch(step).wait()

        @pl.when(step < steps - (HELD - 1))
        def _():
            fetch(step + HELD - 1).start()

        for i in range(TASK_STEP):
            task = step * TASK_STEP + i
            target = jnp.where(task < count[0], targets[task], LEAVES)
            total[target] += jnp.dot(
                held[slot, i], window[sources[task]], preferred_element_type=F32
            )
        return 0

    lax.fori_loop(0, steps, one_step, 0)


def near_field(targets, sources, count, even, odd, ordered, blocks):
    return pl.pallas_call(
        near_kernel,
        out_shape=jax.ShapeDtypeStruct((LEAVES + 1, POINTS, 128), F32),
        in_specs=[
            pl.BlockSpec(memory_space=SMEM),
            pl.BlockSpec(memory_space=SMEM),
            pl.BlockSpec(memory_space=SMEM),
            pl.BlockSpec(memory_space=VMEM),
            pl.BlockSpec(memory_space=VMEM),
            pl.BlockSpec(memory_space=pl.ANY),
            pl.BlockSpec(memory_space=pl.ANY),
        ],
        out_specs=pl.BlockSpec(memory_space=VMEM),
        scratch_shapes=[
            pltpu.VMEM((LEAVES + 2 * HALO, POINTS, 128), BF16),
            pltpu.VMEM((HELD, TASK_STEP, POINTS, POINTS), BF16),
            pltpu.SemaphoreType.DMA,
            pltpu.SemaphoreType.DMA((HELD,)),
        ],
        compiler_params=params(NEAR_MIB),
        cost_estimate=pl.CostEstimate(
            flops=2 * TASKS * POINTS * POINTS * 128,
            bytes_accessed=2 * TASKS * POINTS * POINTS,
            transcendentals=0,
        ),
        name="near_field",
    )(targets, sources, count, even, odd, ordered, blocks)


def result_kernel(*refs):
    perm, fine_slots, coarse_slots = refs[:3]
    own, y_even, y_odd, x_even, x_odd, xy_even, xy_odd = refs[3:10]
    fine, coarse, transfer, basis, near, out = refs[10:16]
    spread, below, above, first_rows, second_rows, table, wide = refs[16:23]
    first_places, second_places, sems, out_sems = refs[23:]
    skeletons = [(own, 0), (y_even, 0), (y_odd, 0), (x_even, 0), (xy_even, 0), (xy_odd, 0)]
    skeletons += [(x_odd, 0), (xy_even, PAIRS), (xy_odd, PAIRS)]
    steps = LEAVES // LEAF_STEP

    def load_places(step, into, sem):
        return pltpu.make_async_copy(perm.at[pl.ds(step * CHUNK, CHUNK)], into, sems.at[sem])

    load_places(0, first_places, 0).start()
    load_places(1, second_places, 1).start()
    low = low_half(RANK)
    keep = (low.astype(F32).astype(BF16), (~low).astype(F32).astype(BF16))
    for a, (source, start) in enumerate(skeletons):

        def part(p, _):
            for z in range(2):
                spread[a * 2 * PAIRS + 2 * p + z] = source[start + p] * keep[z]
            return 0

        lax.fori_loop(0, PAIRS, part, 0, unroll=8)

    def coupled(matrix, slots):
        picked = [spread[slot] for slot in slots]
        return jnp.dot(matrix, jnp.concatenate(picked, axis=0), preferred_element_type=F32)

    def couple(step, _):
        for p in range(4):
            parent = step * 4 + p
            above[parent] = coupled(
                coarse[parent], [coarse_slots[parent, j] for j in range(ENTRIES)]
            )
        for c in range(8):
            leaf = step * 8 + c
            below[leaf] = coupled(fine[leaf], [fine_slots[j, leaf] for j in range(ENTRIES)])
        return 0

    lax.fori_loop(0, LEAVES // 8, couple, 0)

    def fold(halves):
        return halves + pltpu.roll(halves, 64, 1)

    def compute(step, rows):
        for p in range(LEAF_STEP // 2):
            parent = step * (LEAF_STEP // 2) + p
            from_parent = fold(above[parent]).astype(BF16)
            for z in range(2):
                c = 2 * p + z
                leaf = step * LEAF_STEP + c
                local = fold(below[leaf])
                local += jnp.dot(transfer[leaf], from_parent, preferred_element_type=F32)
                far = lax.dot_general(
                    basis[leaf],
                    local.astype(BF16),
                    (((0,), (0,)), ((), ())),
                    preferred_element_type=F32,
                )
                rows[c * POINTS : (c + 1) * POINTS, :] = far + near[leaf]

    def scatter(places, rows):
        for i in range(CHUNK):
            table[pl.ds(places[i], 1), :] = rows[i : i + 1, :]

    compute(0, first_rows)

    def two_steps(pair, _):
        load_places(2 * pair, first_places, 0).wait()
        compute(2 * pair + 1, second_rows)
        scatter(first_places, first_rows)
        more = pair < steps // 2 - 1

        @pl.when(more)
        def _():
            load_places(2 * pair + 2, first_places, 0).start()

        load_places(2 * pair + 1, second_places, 1).wait()
        compute(jnp.minimum(2 * pair + 2, steps - 1), first_rows)
        scatter(second_places, second_rows)

        @pl.when(more)
        def _():
            load_places(2 * pair + 3, second_places, 1).start()

        return 0

    lax.fori_loop(0, steps // 2, two_steps, 0)

    low = low_half(128)
    sends = []
    for n in range(OUT_PARTS):
        width = ROWS // OUT_PARTS
        for c in range(n * width // 128, (n + 1) * width // 128):
            block = table[c * 128 : (c + 1) * 128, :]
            high = block.astype(BF16)
            rest = (block - high.astype(F32)).astype(BF16)
            both = jnp.where(low, high, rest).T.astype(F32)
            wide[:, c * 128 : (c + 1) * 128] = both[:COLS] + both[COLS:]
        span = pl.ds(n * width, width)
        sends.append(pltpu.make_async_copy(wide.at[:, span], out.at[:, span], out_sems.at[n]))
        sends[-1].start()
    for send in sends:
        send.wait()


def result(perm, fine_slots, coarse_slots, skeletons, fine, coarse, transfer, basis, near):
    return pl.pallas_call(
        result_kernel,
        out_shape=jax.ShapeDtypeStruct((COLS, ROWS), F32),
        in_specs=[
            pl.BlockSpec(memory_space=pl.ANY),
            *[pl.BlockSpec(memory_space=SMEM)] * 2,
            *[pl.BlockSpec(memory_space=VMEM)] * 12,
        ],
        out_specs=pl.BlockSpec(memory_space=pl.ANY),
        scratch_shapes=[
            pltpu.VMEM((9 * 2 * PAIRS, RANK, 128), BF16),
            pltpu.VMEM((LEAVES, RANK, 128), F32),
            pltpu.VMEM((PARENTS, RANK, 128), F32),
            pltpu.VMEM((CHUNK, 128), F32),
            pltpu.VMEM((CHUNK, 128), F32),
            pltpu.VMEM((ROWS, 128), F32),
            pltpu.VMEM((COLS, ROWS), F32),
            pltpu.SMEM((CHUNK,), jnp.int32),
            pltpu.SMEM((CHUNK,), jnp.int32),
            pltpu.SemaphoreType.DMA((2,)),
            pltpu.SemaphoreType.DMA((OUT_PARTS,)),
        ],
        compiler_params=params(36),
        name="result",
    )(perm, fine_slots, coarse_slots, *skeletons, fine, coarse, transfer, basis, near)


def join_kernel(first, second, *refs):
    joined, sems = refs[-2:]
    copies = [
        pltpu.make_async_copy(x, joined.at[pl.ds(n * PAIRS, PAIRS)], sems.at[n])
        for n, x in enumerate((first, second))
    ]
    for copy in copies:
        copy.start()
    for copy in copies:
        copy.wait()


def join(first, second, *earlier):
    anywhere = pl.BlockSpec(memory_space=pl.ANY)
    return pl.pallas_call(
        join_kernel,
        out_shape=jax.ShapeDtypeStruct((2 * PAIRS, RANK, 128), BF16),
        in_specs=[anywhere] * (2 + len(earlier)),
        out_specs=anywhere,
        scratch_shapes=[pltpu.SemaphoreType.DMA((2,))],
        compiler_params=params(1),
        name="join",
    )(first, second, *earlier)


def swaps(count, odd):
    pairs = [((i + odd) % count, (i + odd + 1) % count) for i in range(0, count, 2)]
    return [(a, b) for a, b in pairs] + [(b, a) for a, b in pairs]


def swap(x, axis, odd):
    return lax.ppermute(x, axis, swaps(lax.axis_size(axis), odd))


def on_device(
    points_in,
    tree_perm,
    basis,
    transfer,
    couple_fine,
    couple_coarse,
    list_fine,
    list_coarse,
    near_blocks,
    near_target,
    near_source,
    task_count,
):
    basis_rows = basis.transpose(0, 2, 1)
    ordered, own, even_edge, odd_edge, fine_slots, coarse_slots = order_points(
        points_in.T, tree_perm, basis_rows, transfer, list_fine.T, list_coarse
    )
    x_even = swap(own, "gx", 0)
    x_odd = swap(own, "gx", 1)
    y_even = swap(own, "gy", 0)
    even_edge = swap(even_edge, "gy", 0)
    y_odd = swap(own, "gy", 1)
    both = ("gx", "gy")
    line = [(i, i + 1) for i in range(1, lax.axis_size(both) - 1, 2)]
    odd_edge = lax.ppermute(odd_edge, both, line + [(b, a) for a, b in line])
    fine = turn_blocks(couple_fine.transpose(1, 2, 0))
    coarse = turn_blocks(couple_coarse.transpose(1, 2, 0))
    near = near_field(near_target, near_source, task_count, even_edge, odd_edge, ordered, near_blocks)
    x_both = join(x_even, x_odd, y_even, y_odd, even_edge, odd_edge, fine, coarse)
    xy_even = swap(x_both, "gy", 0)
    xy_odd = swap(x_both, "gy", 1)
    skeletons = (own, y_even, y_odd, x_even, x_odd, xy_even, xy_odd)
    out = result(
        tree_perm, fine_slots, coarse_slots, skeletons, fine, coarse, transfer, basis_rows, near
    )
    return out.T


def solution(mesh):
    flat = P(("gx", "gy"))
    return jax.shard_map(
        on_device,
        mesh=mesh,
        in_specs=(flat,) * 12,
        out_specs=flat,
        check_vma=False,
    )
```

```python
import jax
import jax.numpy as jnp
from jax import lax
from jax.experimental import pallas as pl
from jax.experimental.pallas import tpu as pltpu
from jax.sharding import PartitionSpec as P

LEAVES = 32
PARENTS = LEAVES // 2
POINTS = 256
RANK = 64
COLS = 64
ENTRIES = 16
HALO = 2
TASKS = 128
ROWS = LEAVES * POINTS
PAIRS = LEAVES // 2 + PARENTS // 2
EDGE = POINTS // RANK
TASK_STEP = 16
LEAF_STEP = 4
CHUNK = 1024
POINT_PARTS = 4
OUT_PARTS = 8
ORDER_MIB = 60
NEAR_MIB = 36
HELD = 4
PITCH = RANK // 2 + 1

SMEM = pltpu.SMEM
VMEM = pltpu.VMEM
F32 = jnp.float32
BF16 = jnp.bfloat16


def params(mib):
    return pltpu.CompilerParams(vmem_limit_bytes=mib << 20)


def low_half(rows):
    return lax.broadcasted_iota(jnp.int32, (rows, 128), 1) < 64


def swap_halves(x):
    return jnp.concatenate([x[:, 64:], x[:, :64]], axis=1)


def places(lists, clusters, first):
    outer, inner = lax.axis_size("gx"), lax.axis_size("gy")
    gx, gy = lax.axis_index("gx"), lax.axis_index("gy")
    owner = lists >> (clusters.bit_length() - 1)
    step_x = ((owner >> (inner.bit_length() - 1)) - gx) & (outer - 1)
    step_y = (owner - gy) & (inner - 1)
    swap_x = jnp.where(step_x == 1, 1 + (gx & 1), 2 - (gx & 1))
    swap_y = jnp.where(step_y == 1, 1 + (gy & 1), 2 - (gy & 1))
    array = jnp.where(step_x == 0, 0, swap_x) * 3 + jnp.where(step_y == 0, 0, swap_y)
    return array * (2 * PAIRS) + first + (lists & (clusters - 1))


def order_kernel(
    perm,
    points,
    basis,
    transfer,
    fine_lists,
    coarse_lists,
    ordered,
    skeleton,
    even_sent,
    odd_edge,
    fine_slots,
    coarse_slots,
    table,
    even,
    odd,
    fine,
    places_0,
    places_1,
    places_2,
    places_3,
    points_here,
    basis_here,
    transfer_here,
    ordered_here,
    sems,
    out_sems,
):
    width = ROWS // POINT_PARTS

    def part(n):
        span = pl.ds(n * width, width)
        return pltpu.make_async_copy(points.at[:, span], points_here.at[:, span], sems.at[n])

    def load_rows(chunk, into, sem):
        return pltpu.make_async_copy(
            perm.at[pl.ds(chunk * CHUNK, CHUNK)], into, sems.at[POINT_PARTS + sem]
        )

    for n in range(POINT_PARTS):
        part(n).start()
    held = (places_0, places_1, places_2, places_3)
    for n, into in enumerate(held):
        load_rows(n, into, n).start()
    bases = pltpu.make_async_copy(basis, basis_here, sems.at[POINT_PARTS + 4])
    transfers = pltpu.make_async_copy(transfer, transfer_here, sems.at[POINT_PARTS + 5])
    bases.start()
    transfers.start()
    odd[...] = jnp.zeros_like(odd)
    for n in range(POINT_PARTS):
        part(n).wait()
        for c in range(n * width // 128, (n + 1) * width // 128):
            block = points_here[:, c * 128 : (c + 1) * 128].astype(F32)
            table[c * 128 : (c + 1) * 128, :] = jnp.concatenate([block, block], axis=0).T
    bases.wait()

    leaves = CHUNK // POINTS

    def gather(places, into):
        for i in range(CHUNK):
            into[i : i + 1, :] = table[pl.ds(places[i], 1), :]

    def finish(chunk, source):
        for n in range(leaves):
            leaf = chunk * leaves + n
            block = source[n * POINTS : (n + 1) * POINTS, :].astype(BF16)
            ordered_here[leaf] = block
            fine[leaf] = jnp.dot(basis_here[leaf], block, preferred_element_type=F32).astype(BF16)

    def send(chunk):
        span = pl.ds(chunk * leaves, leaves)
        return pltpu.make_async_copy(ordered_here.at[span], ordered.at[span], out_sems.at[chunk])

    chunks = ROWS // CHUNK
    rounds = chunks // len(held)

    def one_round(step, _):
        for n, rows in enumerate(held):
            chunk = step * len(held) + n
            load_rows(chunk, rows, n).wait()
            finish(jnp.maximum(chunk - 1, 0), (odd, even)[n % 2])
            gather(rows, (even, odd)[n % 2])

            @pl.when(step < rounds - 1)
            def _():
                load_rows(chunk + len(held), rows, n).start()

            @pl.when(chunk > 0)
            def _():
                send(chunk - 1).start()

        return 0

    lax.fori_loop(0, rounds, one_round, 0)
    finish(chunks - 1, odd)
    send(chunks - 1).start()

    fine_slots[...] = places(fine_lists[...], LEAVES, 0)
    coarse_slots[...] = places(coarse_lists[...], PARENTS, LEAVES)
    transfers.wait()
    low = low_half(RANK)
    low_points = low_half(POINTS)

    def put(n, block):
        skeleton[n] = block
        even_sent[n] = block

    for p in range(PARENTS):
        put(p, jnp.where(low, fine[2 * p], fine[2 * p + 1]))
    for q in range(PARENTS // 2):
        coarse = []
        for p in (2 * q, 2 * q + 1):
            pair = transfer_here[2 * p : 2 * p + 2].reshape(2 * RANK, RANK)
            stacked = fine[2 * p : 2 * p + 2].reshape(2 * RANK, 128)
            coarse.append(
                lax.dot_general(
                    pair, stacked, (((0,), (0,)), ((), ())), preferred_element_type=F32
                ).astype(BF16)
            )
        put(PARENTS + q, jnp.where(low, coarse[0], coarse[1]))
    odd_here = lax.rem(lax.axis_index("gy"), 2)
    last = (1 - odd_here) * (LEAVES - 2)
    edge = jnp.where(low_points, ordered_here[last], ordered_here[last + 1])
    even_sent[PAIRS:] = edge.reshape(EDGE, RANK, 128)
    last = odd_here * (LEAVES - 2)
    odd_edge[...] = jnp.where(low_points, ordered_here[last], ordered_here[last + 1])
    for chunk in range(ROWS // CHUNK):
        send(chunk).wait()


def order_points(points, perm, basis, transfer, fine_lists, coarse_lists):
    anywhere = pl.BlockSpec(memory_space=pl.ANY)
    vmem = pl.BlockSpec(memory_space=VMEM)
    return pl.pallas_call(
        order_kernel,
        out_shape=(
            jax.ShapeDtypeStruct((LEAVES, POINTS, 128), BF16),
            jax.ShapeDtypeStruct((PAIRS, RANK, 128), BF16),
            jax.ShapeDtypeStruct((PAIRS + EDGE, RANK, 128), BF16),
            jax.ShapeDtypeStruct((POINTS, 128), BF16),
            jax.ShapeDtypeStruct(fine_lists.shape, jnp.int32),
            jax.ShapeDtypeStruct(coarse_lists.shape, jnp.int32),
        ),
        in_specs=[anywhere] * 4 + [vmem] * 2,
        out_specs=(anywhere,) + (vmem,) * 5,
        scratch_shapes=[
            pltpu.VMEM((ROWS, 128), F32),
            pltpu.VMEM((CHUNK, 128), F32),
            pltpu.VMEM((CHUNK, 128), F32),
            pltpu.VMEM((LEAVES, RANK, 128), BF16),
            *[pltpu.SMEM((CHUNK,), jnp.int32)] * 4,
            pltpu.VMEM((COLS, ROWS), BF16),
            pltpu.VMEM((LEAVES, RANK, POINTS), BF16),
            pltpu.VMEM((LEAVES, RANK, RANK), BF16),
            pltpu.VMEM((LEAVES, POINTS, 128), BF16),
            pltpu.SemaphoreType.DMA((POINT_PARTS + 6,)),
            pltpu.SemaphoreType.DMA((ROWS // CHUNK,)),
        ],
        compiler_params=params(ORDER_MIB),
        name="order_points",
    )(perm, points, basis, transfer, fine_lists, coarse_lists)


def turn_kernel(blocks, turned, table):
    half = RANK // 2
    targets = 128 // ENTRIES
    low = low_half(half)

    def tile(n, _):
        entries = pl.ds(pl.multiple_of(n * 128, 128), 128)
        for k in range(half):
            block = jnp.concatenate([blocks[k, :, entries], blocks[k + half, :, entries]], axis=0)
            table[pl.ds(k, 128, stride=PITCH), :] = block.astype(F32).T
        for t in range(targets):
            into = turned.at[n * targets + t]
            for j in range(0, ENTRIES, 2):
                first = table[pl.ds((t * ENTRIES + j) * PITCH, half), :]
                second = table[pl.ds((t * ENTRIES + j + 1) * PITCH, half), :]
                into[:half, j * 64 : (j + 2) * 64] = jnp.where(
                    low, first, pltpu.roll(second, 64, 1)
                ).astype(BF16)
                into[half:, j * 64 : (j + 2) * 64] = jnp.where(
                    low, pltpu.roll(first, 64, 1), second
                ).astype(BF16)
        return 0

    lax.fori_loop(0, blocks.shape[2] // 128, tile, 0)


def turn_blocks(blocks):
    return pl.pallas_call(
        turn_kernel,
        out_shape=jax.ShapeDtypeStruct((blocks.shape[2] // ENTRIES, RANK, ENTRIES * RANK), BF16),
        in_specs=[pl.BlockSpec(memory_space=VMEM)],
        out_specs=pl.BlockSpec(memory_space=VMEM),
        scratch_shapes=[pltpu.VMEM((128 * PITCH, 128), F32)],
        compiler_params=params(24),
        cost_estimate=pl.CostEstimate(
            flops=0, bytes_accessed=6 * blocks.size, transcendentals=0
        ),
        name="turn_blocks",
    )(blocks)


def near_kernel(
    targets, sources, count, even, odd, ordered, blocks, total, window, held, sem, sems
):
    steps = TASKS // TASK_STEP

    def fetch(step):
        slot = lax.rem(step, HELD)
        tasks = pl.ds(step * TASK_STEP, TASK_STEP)
        return pltpu.make_async_copy(blocks.at[tasks], held.at[slot], sems.at[slot])

    copy = pltpu.make_async_copy(ordered, window.at[pl.ds(HALO, LEAVES)], sem)
    copy.start()
    for step in range(HELD - 1):
        fetch(step).start()
    low = low_half(POINTS)
    odd_here = lax.rem(lax.axis_index("gy"), 2)
    from_even = even[PAIRS:].reshape(POINTS, 128)
    after = LEAVES + HALO
    for pair, place in ((from_even, (1 - odd_here) * after), (odd[...], odd_here * after)):
        swapped = swap_halves(pair)
        window[place] = jnp.where(low, pair, swapped)
        window[place + 1] = jnp.where(low, swapped, pair)
    total[...] = jnp.zeros_like(total)
    copy.wait()

    def one_step(step, _):
        slot = lax.rem(step, HELD)
        fetch(step).wait()

        @pl.when(step < steps - (HELD - 1))
        def _():
            fetch(step + HELD - 1).start()

        for i in range(TASK_STEP):
            task = step * TASK_STEP + i
            target = jnp.where(task < count[0], targets[task], LEAVES)
            total[target] += jnp.dot(
                held[slot, i], window[sources[task]], preferred_element_type=F32
            )
        return 0

    lax.fori_loop(0, steps, one_step, 0)


def near_field(targets, sources, count, even, odd, ordered, blocks):
    return pl.pallas_call(
        near_kernel,
        out_shape=jax.ShapeDtypeStruct((LEAVES + 1, POINTS, 128), F32),
        in_specs=[
            pl.BlockSpec(memory_space=SMEM),
            pl.BlockSpec(memory_space=SMEM),
            pl.BlockSpec(memory_space=SMEM),
            pl.BlockSpec(memory_space=VMEM),
            pl.BlockSpec(memory_space=VMEM),
            pl.BlockSpec(memory_space=pl.ANY),
            pl.BlockSpec(memory_space=pl.ANY),
        ],
        out_specs=pl.BlockSpec(memory_space=VMEM),
        scratch_shapes=[
            pltpu.VMEM((LEAVES + 2 * HALO, POINTS, 128), BF16),
            pltpu.VMEM((HELD, TASK_STEP, POINTS, POINTS), BF16),
            pltpu.SemaphoreType.DMA,
            pltpu.SemaphoreType.DMA((HELD,)),
        ],
        compiler_params=params(NEAR_MIB),
        cost_estimate=pl.CostEstimate(
            flops=2 * TASKS * POINTS * POINTS * 128,
            bytes_accessed=2 * TASKS * POINTS * POINTS,
            transcendentals=0,
        ),
        name="near_field",
    )(targets, sources, count, even, odd, ordered, blocks)


def result_kernel(*refs):
    perm, fine_slots, coarse_slots = refs[:3]
    own, y_even, y_odd, x_even, x_odd, xy_even, xy_odd = refs[3:10]
    fine, coarse, transfer, basis, near, out = refs[10:16]
    spread, below, above, first_rows, second_rows, table, wide = refs[16:23]
    first_places, second_places, sems, out_sems = refs[23:]
    skeletons = [(own, 0), (y_even, 0), (y_odd, 0), (x_even, 0), (xy_even, 0), (xy_odd, 0)]
    skeletons += [(x_odd, 0), (xy_even, PAIRS), (xy_odd, PAIRS)]
    steps = LEAVES // LEAF_STEP

    def load_places(step, into, sem):
        return pltpu.make_async_copy(perm.at[pl.ds(step * CHUNK, CHUNK)], into, sems.at[sem])

    load_places(0, first_places, 0).start()
    load_places(1, second_places, 1).start()
    low = low_half(RANK)
    keep = (low.astype(F32).astype(BF16), (~low).astype(F32).astype(BF16))
    for a, (source, start) in enumerate(skeletons):

        def part(p, _):
            for z in range(2):
                spread[a * 2 * PAIRS + 2 * p + z] = source[start + p] * keep[z]
            return 0

        lax.fori_loop(0, PAIRS, part, 0, unroll=8)

    def coupled(matrix, slots):
        picked = [spread[slot] for slot in slots]
        return jnp.dot(matrix, jnp.concatenate(picked, axis=0), preferred_element_type=F32)

    def couple(step, _):
        for p in range(4):
            parent = step * 4 + p
            above[parent] = coupled(
                coarse[parent], [coarse_slots[parent, j] for j in range(ENTRIES)]
            )
        for c in range(8):
            leaf = step * 8 + c
            below[leaf] = coupled(fine[leaf], [fine_slots[j, leaf] for j in range(ENTRIES)])
        return 0

    lax.fori_loop(0, LEAVES // 8, couple, 0)

    def fold(halves):
        return halves + pltpu.roll(halves, 64, 1)

    def compute(step, rows):
        for p in range(LEAF_STEP // 2):
            parent = step * (LEAF_STEP // 2) + p
            from_parent = fold(above[parent]).astype(BF16)
            for z in range(2):
                c = 2 * p + z
                leaf = step * LEAF_STEP + c
                local = fold(below[leaf])
                local += jnp.dot(transfer[leaf], from_parent, preferred_element_type=F32)
                far = lax.dot_general(
                    basis[leaf],
                    local.astype(BF16),
                    (((0,), (0,)), ((), ())),
                    preferred_element_type=F32,
                )
                rows[c * POINTS : (c + 1) * POINTS, :] = far + near[leaf]

    def scatter(places, rows):
        for i in range(CHUNK):
            table[pl.ds(places[i], 1), :] = rows[i : i + 1, :]

    compute(0, first_rows)

    def two_steps(pair, _):
        load_places(2 * pair, first_places, 0).wait()
        compute(2 * pair + 1, second_rows)
        scatter(first_places, first_rows)
        more = pair < steps // 2 - 1

        @pl.when(more)
        def _():
            load_places(2 * pair + 2, first_places, 0).start()

        load_places(2 * pair + 1, second_places, 1).wait()
        compute(jnp.minimum(2 * pair + 2, steps - 1), first_rows)
        scatter(second_places, second_rows)

        @pl.when(more)
        def _():
            load_places(2 * pair + 3, second_places, 1).start()

        return 0

    lax.fori_loop(0, steps // 2, two_steps, 0)

    low = low_half(128)
    sends = []
    for n in range(OUT_PARTS):
        width = ROWS // OUT_PARTS
        for c in range(n * width // 128, (n + 1) * width // 128):
            block = table[c * 128 : (c + 1) * 128, :]
            high = block.astype(BF16)
            rest = (block - high.astype(F32)).astype(BF16)
            both = jnp.where(low, high, rest).T.astype(F32)
            wide[:, c * 128 : (c + 1) * 128] = both[:COLS] + both[COLS:]
        span = pl.ds(n * width, width)
        sends.append(pltpu.make_async_copy(wide.at[:, span], out.at[:, span], out_sems.at[n]))
        sends[-1].start()
    for send in sends:
        send.wait()


def result(perm, fine_slots, coarse_slots, skeletons, fine, coarse, transfer, basis, near):
    return pl.pallas_call(
        result_kernel,
        out_shape=jax.ShapeDtypeStruct((COLS, ROWS), F32),
        in_specs=[
            pl.BlockSpec(memory_space=pl.ANY),
            *[pl.BlockSpec(memory_space=SMEM)] * 2,
            *[pl.BlockSpec(memory_space=VMEM)] * 12,
        ],
        out_specs=pl.BlockSpec(memory_space=pl.ANY),
        scratch_shapes=[
            pltpu.VMEM((9 * 2 * PAIRS, RANK, 128), BF16),
            pltpu.VMEM((LEAVES, RANK, 128), F32),
            pltpu.VMEM((PARENTS, RANK, 128), F32),
            pltpu.VMEM((CHUNK, 128), F32),
            pltpu.VMEM((CHUNK, 128), F32),
            pltpu.VMEM((ROWS, 128), F32),
            pltpu.VMEM((COLS, ROWS), F32),
            pltpu.SMEM((CHUNK,), jnp.int32),
            pltpu.SMEM((CHUNK,), jnp.int32),
            pltpu.SemaphoreType.DMA((2,)),
            pltpu.SemaphoreType.DMA((OUT_PARTS,)),
        ],
        compiler_params=params(36),
        name="result",
    )(perm, fine_slots, coarse_slots, *skeletons, fine, coarse, transfer, basis, near)


def join_kernel(first, second, *refs):
    joined, sems = refs[-2:]
    copies = [
        pltpu.make_async_copy(x, joined.at[pl.ds(n * PAIRS, PAIRS)], sems.at[n])
        for n, x in enumerate((first, second))
    ]
    for copy in copies:
        copy.start()
    for copy in copies:
        copy.wait()


def join(first, second, *earlier):
    anywhere = pl.BlockSpec(memory_space=pl.ANY)
    return pl.pallas_call(
        join_kernel,
        out_shape=jax.ShapeDtypeStruct((2 * PAIRS, RANK, 128), BF16),
        in_specs=[anywhere] * (2 + len(earlier)),
        out_specs=anywhere,
        scratch_shapes=[pltpu.SemaphoreType.DMA((2,))],
        compiler_params=params(1),
        name="join",
    )(first, second, *earlier)


def swaps(count, odd):
    pairs = [((i + odd) % count, (i + odd + 1) % count) for i in range(0, count, 2)]
    return [(a, b) for a, b in pairs] + [(b, a) for a, b in pairs]


def swap(x, axis, odd):
    return lax.ppermute(x, axis, swaps(lax.axis_size(axis), odd))


def on_device(
    points_in,
    tree_perm,
    basis,
    transfer,
    couple_fine,
    couple_coarse,
    list_fine,
    list_coarse,
    near_blocks,
    near_target,
    near_source,
    task_count,
):
    basis_rows = basis.transpose(0, 2, 1)
    ordered, own, even_sent, odd_edge, fine_slots, coarse_slots = order_points(
        points_in.T, tree_perm, basis_rows, transfer, list_fine.T, list_coarse
    )
    x_even = swap(own, "gx", 0)
    x_odd = swap(own, "gx", 1)
    y_even = swap(even_sent, "gy", 0)
    y_odd = swap(own, "gy", 1)
    both = ("gx", "gy")
    line = [(i, i + 1) for i in range(1, lax.axis_size(both) - 1, 2)]
    odd_edge = lax.ppermute(odd_edge, both, line + [(b, a) for a, b in line])
    fine = turn_blocks(couple_fine.transpose(1, 2, 0))
    coarse = turn_blocks(couple_coarse.transpose(1, 2, 0))
    near = near_field(near_target, near_source, task_count, y_even, odd_edge, ordered, near_blocks)
    x_both = join(x_even, x_odd, y_even, y_odd, odd_edge, fine, coarse)
    xy_even = swap(x_both, "gy", 0)
    xy_odd = swap(x_both, "gy", 1)
    skeletons = (own, y_even, y_odd, x_even, x_odd, xy_even, xy_odd)
    out = result(
        tree_perm, fine_slots, coarse_slots, skeletons, fine, coarse, transfer, basis_rows, near
    )
    return out.T


def solution(mesh):
    flat = P(("gx", "gy"))
    return jax.shard_map(
        on_device,
        mesh=mesh,
        in_specs=(flat,) * 12,
        out_specs=flat,
        check_vma=False,
    )
```
